32 devices in a mesh: row: 4 (over x, core), col: 8 (over z, y).
Axes of the slice: x: 2, y: 2, z: 4, core: 2. Of those that a mesh axis runs over, the one named last changes fastest.
Arguments:
- vectors: float32 [1792, 128], P('row'), may hold values from -6 to 6
- tiles: float32 [4, 8, 10, 56, 56], P('row', 'col'), may hold values from -0.1875 to 0.1875
- tile_pos: int32 [4, 8, 2, 10], P('row', 'col'), may hold values from 0 to 7, as said below
- diag_blocks: float32 [32, 56, 56], P(('row', 'col')), as said below
Outputs:
- filtered: float32 [1792, 128], P('row')
The draws below stay inside these ranges and needn't reach their ends.
Inputs may be any that keep to these rules, and one draw needn't show every extreme that they name: For each device position (r, c), tile_pos[r, c, 0, t] is below 8 and tile_pos[r, c, 1, t] below 4; no two entries of one device are equal pairs; with I and J as in the reference program, I differs from J, and I < J exactly when I + J is odd, so no block and its mirror are both stored. Where 10 + 1 <= 8, the stored blocks of the device at (r, c) lie in 10 different local block rows, none of them among c * 1 to c + 1 - 1. `diag_blocks`: every diagonal block is symmetric.
All inputs are finite; a program needn't handle non-finite values.
Results may differ from the reference program's by a relative error of at most 0.00011.
Values sent between devices are 32-bit elements; how exact they have to be, the bound alone decides.
A program may use at most 64 MiB of HBM per device.

```python
import math
import jax
import jax.numpy as jnp
from jax import lax

ORB = 56
VECS = 128
STORED_ROW = 10
DEGREE = 3
BLK_SLICE = 1
BLOCKS = 32
TILES_DEV = 10
N_ROW = 4
N_COL = 8


def draw_tile_pos(key, part):
    key = jax.random.fold_in(key, 11)
    group_rows = BLK_SLICE * N_COL
    group_cols = BLK_SLICE * N_ROW
    pairs_total = group_rows * group_cols
    spread = 2 * group_rows + 2
    far_global = (N_ROW - 1) * group_rows
    forced_row = BLK_SLICE + (far_global + 1 + BLK_SLICE) % 2
    forced_col = (N_ROW - 1) * BLK_SLICE

    def one_device(device_key, row_index, col_index):
        order_key, rank_key = jax.random.split(device_key)
        local_row = jnp.arange(group_rows, dtype=jnp.int32)[:, None]
        local_col = jnp.arange(group_cols, dtype=jnp.int32)[None, :]
        global_row = row_index * group_rows + local_row
        global_col = local_col // BLK_SLICE * group_rows + col_index * BLK_SLICE + local_col % BLK_SLICE
        odd_sum = (global_row + global_col) % 2 == 1
        allowed = (global_row != global_col) & ((global_row < global_col) == odd_sum)
        first_device = (row_index == 0) & (col_index == 0)
        last_device = (row_index == 0) & (col_index == N_COL - 1)
        forced = first_device & (local_row == forced_row) & (local_col == forced_col)
        ranking = jax.random.permutation(rank_key, pairs_total).astype(jnp.int32).reshape(group_rows, group_cols)
        ranking = jnp.where(forced, -1, ranking)
        earlier = allowed[:, None, :] & (ranking[:, None, :] < ranking[:, :, None])
        within = jnp.sum(earlier.astype(jnp.int32), axis=2)
        rows_flat = jnp.arange(group_rows, dtype=jnp.int32)
        priority = jax.random.permutation(order_key, group_rows).astype(jnp.int32)
        own_rows = rows_flat // BLK_SLICE == col_index
        priority = jnp.where(own_rows, priority + group_rows, priority)
        priority = jnp.where(first_device & (rows_flat == group_rows - 1), -1, priority)
        priority = jnp.where(last_device & (rows_flat == 0), -2, priority)
        priority = jnp.where(first_device & (rows_flat == forced_row), -3, priority)
        priority = priority + 2
        flat_index = jnp.arange(pairs_total, dtype=jnp.int32).reshape(group_rows, group_cols)
        scores = jnp.where(allowed, within * spread + priority[:, None], spread * group_cols + flat_index)
        chosen = jnp.argsort(scores.reshape(-1), stable=True)[:TILES_DEV].astype(jnp.int32)
        return jnp.stack([chosen // group_cols, chosen % group_cols]).astype(jnp.int32)
    device_keys = jax.random.split(key, N_ROW * N_COL)
    row_ids = jnp.repeat(jnp.arange(N_ROW, dtype=jnp.int32), N_COL)
    col_ids = jnp.tile(jnp.arange(N_COL, dtype=jnp.int32), N_ROW)
    result = jax.vmap(one_device)(device_keys, row_ids, col_ids)
    return result.reshape(N_ROW, N_COL, 2, TILES_DEV).astype(jnp.int32)


def draw_diag_blocks(key, part):
    key = jax.random.fold_in(key, 23)
    noise_key, level_key = jax.random.split(key)
    noise = jax.random.normal(noise_key, (BLOCKS, ORB, ORB), jnp.float32)
    levels = jax.random.uniform(level_key, (BLOCKS, ORB), jnp.float32, 0.0, 5.0)
    symmetric = (noise + jnp.swapaxes(noise, 1, 2)) * (0.5 / math.sqrt(ORB))
    identity = jnp.eye(ORB, dtype=jnp.float32)
    return (symmetric + identity[None, :, :] * levels[:, :, None]).astype(jnp.float32)


def shard_levels(key, extent, cuts, least, largest):
    loudness = 1.0
    for axis_at, blocks in cuts:
        heights = jax.random.uniform(jax.random.fold_in(jax.random.fold_in(key, 6), axis_at), (blocks,), jnp.float32, least / len(cuts), largest / len(cuts))
        loudness = loudness * jnp.repeat(jnp.exp(heights), extent[axis_at] // blocks).reshape((-1,) + (1,) * (len(extent) - 1 - axis_at))
    return loudness


def bell_draw(stream_key, extent, width, reach, cuts=(), kind=jnp.bfloat16):
    values = jax.random.normal(stream_key, extent, jnp.float32) * width
    if len(cuts) > 0:
        values = shard_levels(stream_key, extent, cuts, -0.22, 0.18) * values
    return jnp.clip(values, min=-reach, max=reach).astype(kind)


def setup_inputs(seed: int = 0) -> dict:
    splits = jax.random.split(jax.random.key(seed), 5)
    vectors = bell_draw(splits[0], (BLOCKS * ORB, VECS), 1.0, 6.0, ((0, 4),), jnp.float32)
    tiles = bell_draw(splits[1], (N_ROW, N_COL, TILES_DEV, ORB, ORB), (2 * STORED_ROW * ORB) ** -0.5, 0.1875, ((0, 4), (1, 8)), jnp.float32)
    tile_pos = draw_tile_pos(jax.random.fold_in(splits[4], 71), 0)
    diag_blocks = draw_diag_blocks(jax.random.fold_in(splits[4], 71), 0)
    return {"vectors": vectors, "tiles": tiles, "tile_pos": tile_pos, "diag_blocks": diag_blocks}


filter_low = 0.0
filter_high = 8.0


def apply_operator(field, tiles, tile_pos, diag_blocks):
    blocks = field.reshape(-1, ORB, VECS)
    row_blocks = BLK_SLICE * N_COL
    total_blocks = row_blocks * N_ROW
    rows_local = tile_pos[:, :, 0, :]
    cols_local = tile_pos[:, :, 1, :]
    group = jnp.arange(N_ROW, dtype=jnp.int32)[:, None, None]
    column = jnp.arange(N_COL, dtype=jnp.int32)[None, :, None]
    global_rows = (group * row_blocks + rows_local).reshape(-1).astype(jnp.int32)
    global_cols = ((cols_local // BLK_SLICE) * row_blocks + column * BLK_SLICE + cols_local % BLK_SLICE).reshape(-1).astype(jnp.int32)
    tile_data = tiles.reshape(-1, ORB, ORB)
    direct = jnp.einsum("tab,tbk->tak", tile_data, blocks[global_cols], precision=lax.Precision.HIGHEST)
    direct_sum = jax.ops.segment_sum(direct, global_rows, num_segments=total_blocks)
    mirror = jnp.einsum("tba,tbk->tak", tile_data, blocks[global_rows], precision=lax.Precision.HIGHEST)
    mirror_sum = jax.ops.segment_sum(mirror, global_cols, num_segments=total_blocks)
    diagonal = jnp.einsum("sab,sbk->sak", diag_blocks, blocks, precision=lax.Precision.HIGHEST)
    return (direct_sum + mirror_sum + diagonal).reshape(field.shape)


def reference(vectors, tiles, tile_pos, diag_blocks):
    centre = 0.5 * (filter_high + filter_low)
    half_width = 0.5 * (filter_high - filter_low)
    previous = vectors
    current = (apply_operator(vectors, tiles, tile_pos, diag_blocks) - centre * vectors) / half_width
    for step in range(DEGREE - 1):
        image = apply_operator(current, tiles, tile_pos, diag_blocks)
        following = 2.0 * (image - centre * current) / half_width - previous
        previous, current = current, following
    return current
```

```python
import functools

import jax
import jax.numpy as jnp
from jax import lax
from jax.experimental import pallas as pl
from jax.experimental.pallas import tpu as pltpu
from jax.sharding import PartitionSpec as P

DEGREE = 3
MESH = pl.DeviceIdType.MESH

filter_low = 0.0
filter_high = 8.0


def halves(value):
    high = value.astype(jnp.bfloat16)
    return high, (value - high.astype(jnp.float32)).astype(jnp.bfloat16)


def product(left_high, left_low, right):
    right_high, right_low = halves(right)
    dot = functools.partial(jnp.dot, preferred_element_type=jnp.float32)
    return dot(left_high, right_high) + (dot(left_high, right_low) + dot(left_low, right_high))


def kernel(
    n_row, n_col, slot_ref, vectors_ref, tiles_ref, diag_ref, out_ref,
    dense, dense_h, dense_l, mirror_h, mirror_l,
    col_field, row_field, direct, mirror, direct_in, mirror_in, send_sem, recv_sem,
):
    orb = diag_ref.shape[0]
    rows, cols = n_col * orb, n_row * orb
    r, c = lax.axis_index("row"), lax.axis_index("col")
    row_peers = [lax.rem(r + d, n_row) for d in range(1, n_row)]
    col_peers = [lax.rem(c + d, n_col) for d in range(1, n_col)]

    def block(index):
        return pl.ds(pl.multiple_of(index * orb, 8), orb)

    barrier = pltpu.get_barrier_semaphore()
    for peer in row_peers:
        pl.semaphore_signal(barrier, inc=1, device_id=(peer, c), device_id_type=MESH)
    for peer in col_peers:
        pl.semaphore_signal(barrier, inc=1, device_id=(r, peer), device_id_type=MESH)

    def send(kind, step, source, target, device):
        pltpu.make_async_remote_copy(
            src_ref=source, dst_ref=target,
            send_sem=send_sem.at[kind, step], recv_sem=recv_sem.at[kind, step],
            device_id=device, device_id_type=MESH,
        ).start()

    def awaited(kind, step, region):
        return pltpu.make_async_remote_copy(
            src_ref=region, dst_ref=region,
            send_sem=send_sem.at[kind, step], recv_sem=recv_sem.at[kind, step],
            device_id=(r, c), device_id_type=MESH,
        )

    def region_of(kind, step):
        if kind == 0:
            return col_field.at[step, pl.ds(0, cols - orb)]
        if kind == 1:
            return direct_in.at[step]
        if kind == 2:
            return mirror_in.at[step]
        if step == DEGREE - 1:
            return out_ref.at[pl.ds(0, rows - orb)]
        return row_field.at[step, pl.ds(0, rows - orb)]

    pl.semaphore_wait(barrier, n_row + n_col - 2)

    own = vectors_ref[block(c), :]
    col_field[0, block(r), :] = own
    for peer in row_peers:
        send(0, 0, vectors_ref.at[block(c)], col_field.at[0, block(r)], (peer, c))

    dense[...] = jnp.zeros_like(dense)

    def fill(i, carry):
        parts = []
        for j in range(n_row):
            slot = slot_ref[i, j]
            tile = tiles_ref[jnp.maximum(slot - 1, 0)]
            parts.append(jnp.where(slot > 0, tile, 0.0))
        dense[block(i), pl.ds(0, cols)] = jnp.concatenate(parts, axis=1)
        return carry

    lax.fori_loop(0, n_col, fill, 0)
    whole = dense[...]
    dense_h[...], dense_l[...] = halves(whole)
    mirror_h[...], mirror_l[...] = halves(whole.T)
    diag_h, diag_l = halves(diag_ref[...])

    centre = 0.5 * (filter_high + filter_low)
    half_width = 0.5 * (filter_high - filter_low)
    previous = None
    for step in range(DEGREE):
        awaited(0, step, region_of(0, step)).wait_recv()
        direct[step] = product(
            dense_h[pl.ds(0, rows), pl.ds(0, cols)], dense_l[pl.ds(0, rows), pl.ds(0, cols)], col_field[step]
        )
        for d, peer in enumerate(col_peers):
            send(1, step, direct.at[step, block(peer)], direct_in.at[step, d], (r, peer))
        if step == 0:
            field = vectors_ref[...]
        else:
            awaited(3, step - 1, region_of(3, step - 1)).wait_recv()
            field = row_field[step - 1]
        mirror[step] = product(
            mirror_h[pl.ds(0, cols), pl.ds(0, rows)], mirror_l[pl.ds(0, cols), pl.ds(0, rows)], field
        )
        for d, peer in enumerate(row_peers):
            send(2, step, mirror.at[step, block(peer)], mirror_in.at[step, d], (peer, c))
        image = product(diag_h, diag_l, own) + direct[step, block(c), :] + mirror[step, block(r), :]
        awaited(2, step, region_of(2, step)).wait_recv()
        for d in range(n_row - 1):
            image = image + mirror_in[step, d]
        awaited(1, step, region_of(1, step)).wait_recv()
        for d in range(n_col - 1):
            image = image + direct_in[step, d]
        shifted = (image - centre * own) / half_width
        following = shifted if step == 0 else 2.0 * shifted - previous
        previous, own = own, following
        if step < DEGREE - 1:
            col_field[step + 1, block(r), :] = own
            row_field[step, block(c), :] = own
            for peer in row_peers:
                send(0, step + 1, row_field.at[step, block(c)], col_field.at[step + 1, block(r)], (peer, c))
            for peer in col_peers:
                send(3, step, row_field.at[step, block(c)], row_field.at[step, block(c)], (r, peer))
        else:
            out_ref[block(c), :] = own
            for peer in col_peers:
                send(3, step, out_ref.at[block(c)], out_ref.at[block(c)], (r, peer))
    awaited(3, DEGREE - 1, region_of(3, DEGREE - 1)).wait_recv()
    for kind in range(4):
        for step in range(DEGREE):
            awaited(kind, step, region_of(kind, step)).wait_send()


def up(value, unit):
    return (value + unit - 1) // unit * unit


def body(n_row, n_col, vectors, tiles, tile_pos, diag_blocks):
    tile_data = tiles[0, 0]
    stored, orb, _ = tile_data.shape
    width = vectors.shape[1]
    rows, cols = n_col * orb, n_row * orb
    at_row = tile_pos[0, 0, 0][:, None, None] == jnp.arange(n_col, dtype=jnp.int32)[None, :, None]
    at_col = tile_pos[0, 0, 1][:, None, None] == jnp.arange(n_row, dtype=jnp.int32)[None, None, :]
    number = jnp.arange(1, stored + 1, dtype=jnp.int32)[:, None, None]
    slots = jnp.sum(jnp.where(at_row & at_col, number, 0), axis=0)
    vmem = pl.BlockSpec(memory_space=pltpu.VMEM)
    f32, bf16 = jnp.float32, jnp.bfloat16
    tall, broad = up(rows, 128), up(cols, 128)
    return pl.pallas_call(
        functools.partial(kernel, n_row, n_col),
        out_shape=jax.ShapeDtypeStruct((rows, width), f32),
        in_specs=[pl.BlockSpec(memory_space=pltpu.SMEM), vmem, vmem, vmem],
        out_specs=vmem,
        scratch_shapes=[
            pltpu.VMEM((tall, broad), f32),
            pltpu.VMEM((tall, broad), bf16),
            pltpu.VMEM((tall, broad), bf16),
            pltpu.VMEM((broad, tall), bf16),
            pltpu.VMEM((broad, tall), bf16),
            pltpu.VMEM((DEGREE, cols, width), f32),
            pltpu.VMEM((DEGREE - 1, rows, width), f32),
            pltpu.VMEM((DEGREE, rows, width), f32),
            pltpu.VMEM((DEGREE, cols, width), f32),
            pltpu.VMEM((DEGREE, n_col - 1, orb, width), f32),
            pltpu.VMEM((DEGREE, n_row - 1, orb, width), f32),
            pltpu.SemaphoreType.DMA((4, DEGREE)),
            pltpu.SemaphoreType.DMA((4, DEGREE)),
        ],
        compiler_params=pltpu.CompilerParams(
            collective_id=0, has_side_effects=True, vmem_limit_bytes=48 * 1024 * 1024
        ),
        cost_estimate=pl.CostEstimate(
            flops=4 * DEGREE * rows * cols * width, bytes_accessed=8 * rows * width, transcendentals=0
        ),
    )(slots, vectors, tile_data, diag_blocks[0])


def solution(mesh):
    return jax.shard_map(
        functools.partial(body, mesh.shape["row"], mesh.shape["col"]),
        mesh=mesh,
        in_specs=(
            P("row", None),
            P("row", "col", None, None, None),
            P("row", "col", None, None),
            P(("row", "col"), None, None),
        ),
        out_specs=P("row", None),
        check_vma=False,
    )
```

```python
import functools

import jax
import jax.numpy as jnp
from jax import lax
from jax.experimental import pallas as pl
from jax.experimental.pallas import tpu as pltpu
from jax.sharding import PartitionSpec as P

DEGREE = 3
MESH = pl.DeviceIdType.MESH

filter_low = 0.0
filter_high = 8.0


def halves(value):
    high = value.astype(jnp.bfloat16)
    return high, (value - high.astype(jnp.float32)).astype(jnp.bfloat16)


def product(left_high, left_low, right):
    right_high, right_low = halves(right)
    dot = functools.partial(jnp.dot, preferred_element_type=jnp.float32)
    return dot(left_high, right_high) + (dot(left_high, right_low) + dot(left_low, right_high))


def mix(fixed, rolled, field, left):
    far = pltpu.roll(field, field.shape[1] // 2, 1)
    both = product(fixed[0][...], fixed[1][...], field) + product(rolled[0][...], rolled[1][...], far)
    count = both.shape[0] // 2
    return jnp.where(left, both[:count], both[count:])


def kernel(
    n_row, n_col, slot_hbm, vectors_hbm, tiles_hbm, diag_hbm, out_ref,
    slots, slots_smem, vectors, tiles, diags, packed, dense,
    down_fixed_h, down_fixed_l, down_rolled_h, down_rolled_l,
    up_fixed_h, up_fixed_l, up_rolled_h, up_rolled_l,
    col_field, row_field, final, direct, mirror, direct_in, mirror_in,
    load_sem, send_sem, recv_sem,
):
    orb = diag_hbm.shape[0]
    width = vectors.shape[1]
    stored = tiles.shape[1]
    half = n_col // 2
    rows, cols = half * orb, n_row * orb
    r, c = lax.axis_index("row"), lax.axis_index("col")
    h, m = c // half, c % half
    other = 1 - h
    partner = other * half + m
    row_peers = [lax.rem(r + d, n_row) for d in range(1, n_row)]
    col_slots = [lax.rem(m + d, half) for d in range(1, half)]
    left = lax.broadcasted_iota(jnp.int32, (1, width), 1) < width // 2

    def block(index):
        return pl.ds(pl.multiple_of(index * orb, 8), orb)

    loads = [
        pltpu.make_async_copy(slot_hbm, slots.at[0], load_sem.at[0]),
        pltpu.make_async_copy(vectors_hbm, vectors, load_sem.at[1]),
        pltpu.make_async_copy(tiles_hbm, tiles.at[0], load_sem.at[2]),
        pltpu.make_async_copy(diag_hbm, diags.at[0], load_sem.at[3]),
        pltpu.make_async_copy(slot_hbm, slots_smem.at[0], load_sem.at[4]),
    ]
    for load in loads:
        load.start()

    barrier = pltpu.get_barrier_semaphore()
    for peer in row_peers:
        pl.semaphore_signal(barrier, inc=1, device_id=(peer, c), device_id_type=MESH)
    for slot in col_slots:
        pl.semaphore_signal(barrier, inc=1, device_id=(r, h * half + slot), device_id_type=MESH)
    pl.semaphore_signal(barrier, inc=1, device_id=(r, partner), device_id_type=MESH)

    def copy(kind, step, source, target, device):
        return pltpu.make_async_remote_copy(
            src_ref=source, dst_ref=target,
            send_sem=send_sem.at[kind, step], recv_sem=recv_sem.at[kind, step],
            device_id=device, device_id_type=MESH,
        )

    def region_of(kind, step):
        if kind == 0:
            return col_field.at[step, pl.ds(0, cols - orb)]
        if kind == 1:
            return direct_in.at[step]
        if kind == 2:
            return mirror_in.at[step]
        if kind == 3 and step < DEGREE - 1:
            return row_field.at[step, pl.ds(0, rows - orb)]
        if kind == 3 or step == 3:
            return final.at[0, pl.ds(0, rows - orb)]
        if step == 0:
            return packed.at[1]
        if step == 1:
            return slots.at[1]
        return final.at[0, pl.ds(0, orb)]

    def awaited(kind, step):
        region = region_of(kind, step)
        return copy(kind, step, region, region, (r, c))

    loads[2].wait()
    loads[3].wait()
    part = (width - 2 * orb) // 8 * 8
    for k in range(stored // 2):
        pieces = [tiles[0, 2 * k], tiles[0, 2 * k + 1]]
        if k * part < orb:
            share = min(part, orb - k * part)
            pieces.append(diags[0, :, pl.ds(k * part, share)])
            if share < part:
                pieces.append(jnp.zeros((orb, part - share), jnp.float32))
        else:
            pieces.append(jnp.zeros((orb, part), jnp.float32))
        packed[0, k] = jnp.concatenate(pieces, axis=1)
    loads[0].wait()
    loads[1].wait()
    top, bottom = vectors[pl.ds(0, rows), :], vectors[pl.ds(rows, rows), :]
    first = jnp.where(h == 0, top, pltpu.roll(top, width // 2, 1))
    second = jnp.where(h == 0, pltpu.roll(bottom, width // 2, 1), bottom)
    row_field[DEGREE - 1] = jnp.where(left, first, second)
    own = row_field[DEGREE - 1, block(m), :]
    col_field[0, block(r), :] = own

    pl.semaphore_wait(barrier, n_row + half - 1)

    copy(4, 1, slots.at[0], slots.at[1], (r, partner)).start()
    copy(4, 0, packed.at[0], packed.at[1], (r, partner)).start()
    for peer in row_peers:
        copy(0, 0, row_field.at[DEGREE - 1, block(m)], col_field.at[0, block(r)], (peer, c)).start()

    dense[...] = jnp.zeros_like(dense)
    loads[4].wait()

    def fill(source, place):
        for a in range(2):
            def one(i, carry):
                parts = []
                for j in range(n_row):
                    slot = slots_smem[source, a * half + i, j]
                    tile = tiles[source, jnp.maximum(slot - 1, 0)]
                    parts.append(jnp.where(slot > 0, tile, 0.0))
                dense[a, place, block(i), pl.ds(0, cols)] = jnp.concatenate(parts, axis=1)
                return carry

            lax.fori_loop(0, half, one, 0)

    fill(0, h)
    awaited(4, 1).wait_recv()
    other_slots = pltpu.make_async_copy(slots.at[1], slots_smem.at[1], load_sem.at[5])
    other_slots.start()
    other_slots.wait()
    awaited(4, 0).wait_recv()
    pieces = []
    for k in range(stored // 2):
        pair = packed[1, k]
        tiles[1, 2 * k] = pair[:, :orb]
        tiles[1, 2 * k + 1] = pair[:, orb : 2 * orb]
        if k * part < orb:
            pieces.append(pair[:, 2 * orb : 2 * orb + min(part, orb - k * part)])
    diags[1] = jnp.concatenate(pieces, axis=1)
    fill(1, other)

    near, far = pl.ds(0, rows), pl.ds(rows, rows)
    for target_h, target_l, parts in (
        (down_fixed_h, down_fixed_l, ((0, 0), (1, 1))), (down_rolled_h, down_rolled_l, ((0, 1), (1, 0))),
    ):
        for place, (a, b) in zip((near, far), parts):
            target_h[place, :], target_l[place, :] = halves(dense[a, b, pl.ds(0, rows), pl.ds(0, cols)])
    near, far = pl.ds(0, cols), pl.ds(cols, cols)
    for target_h, target_l, parts in (
        (up_fixed_h, up_fixed_l, ((0, 0), (1, 1))), (up_rolled_h, up_rolled_l, ((1, 0), (0, 1))),
    ):
        for place, (a, b) in zip((near, far), parts):
            target_h[place, :], target_l[place, :] = halves(dense[a, b].T[:cols, :rows])
    diag_left = halves(jnp.where(h == 0, diags[0], diags[1]))
    diag_right = halves(jnp.where(h == 0, diags[1], diags[0]))

    centre = 0.5 * (filter_high + filter_low)
    half_width = 0.5 * (filter_high - filter_low)
    previous = None
    for step in range(DEGREE):
        awaited(0, step).wait_recv()
        direct[step] = mix((down_fixed_h, down_fixed_l), (down_rolled_h, down_rolled_l), col_field[step], left)
        for d, slot in enumerate(col_slots):
            copy(1, step, direct.at[step, block(slot)], direct_in.at[step, d], (r, h * half + slot)).start()
        if step == 0:
            field = row_field[DEGREE - 1]
        else:
            awaited(3, step - 1).wait_recv()
            field = row_field[step - 1]
        mirror[step] = mix((up_fixed_h, up_fixed_l), (up_rolled_h, up_rolled_l), field, left)
        for d, peer in enumerate(row_peers):
            copy(2, step, mirror.at[step, block(peer)], mirror_in.at[step, d], (peer, c)).start()
        image = jnp.where(left, product(*diag_left, own), product(*diag_right, own))
        image = image + direct[step, block(m), :] + mirror[step, block(r), :]
        awaited(1, step).wait_recv()
        for d in range(half - 1):
            image = image + direct_in[step, d]
        awaited(2, step).wait_recv()
        for d in range(n_row - 1):
            image = image + mirror_in[step, d]
        shifted = (image - centre * own) / half_width
        following = shifted if step == 0 else 2.0 * shifted - previous
        previous, own = own, following
        if step < DEGREE - 1:
            col_field[step + 1, block(r), :] = own
            row_field[step, block(m), :] = own
            mine = row_field.at[step, block(m)]
            for peer in row_peers:
                copy(0, step + 1, mine, col_field.at[step + 1, block(r)], (peer, c)).start()
            for slot in col_slots:
                copy(3, step, mine, mine, (r, h * half + slot)).start()
    final[h, block(m), :] = own
    mine, theirs = final.at[h, block(m)], final.at[other, block(m)]
    copy(4, 2, mine, mine, (r, partner)).start()
    for slot in col_slots:
        copy(3, DEGREE - 1, mine, mine, (r, h * half + slot)).start()
    awaited(4, 2).wait_recv()
    for slot in col_slots:
        copy(4, 3, theirs, theirs, (r, h * half + slot)).start()
    awaited(3, DEGREE - 1).wait_recv()
    awaited(4, 3).wait_recv()
    low, high = final[0], final[1]
    out_ref[pl.ds(0, rows), :] = jnp.where(left, low, pltpu.roll(high, width // 2, 1))
    out_ref[pl.ds(rows, rows), :] = jnp.where(left, pltpu.roll(low, width // 2, 1), high)
    for kind in range(5):
        for step in range(4 if kind == 4 else DEGREE):
            awaited(kind, step).wait_send()


def up(value, unit):
    return (value + unit - 1) // unit * unit


def body(n_row, n_col, vectors, tiles, tile_pos, diag_blocks):
    tile_data = tiles[0, 0]
    stored, orb, _ = tile_data.shape
    width = vectors.shape[1]
    half = n_col // 2
    rows, cols = half * orb, n_row * orb
    at_row = tile_pos[0, 0, 0][:, None, None] == jnp.arange(n_col, dtype=jnp.int32)[None, :, None]
    at_col = tile_pos[0, 0, 1][:, None, None] == jnp.arange(128, dtype=jnp.int32)[None, None, :]
    number = jnp.arange(1, stored + 1, dtype=jnp.int32)[:, None, None]
    slots = jnp.sum(jnp.where(at_row & at_col, number, 0), axis=0)
    hbm = pl.BlockSpec(memory_space=pl.ANY)
    f32, bf16, i32 = jnp.float32, jnp.bfloat16, jnp.int32
    down = pltpu.VMEM((2 * rows, cols), bf16)
    upward = pltpu.VMEM((2 * cols, rows), bf16)
    return pl.pallas_call(
        functools.partial(kernel, n_row, n_col),
        out_shape=jax.ShapeDtypeStruct((2 * rows, width), f32),
        in_specs=[hbm, hbm, hbm, hbm],
        out_specs=pl.BlockSpec(memory_space=pltpu.VMEM),
        scratch_shapes=[
            pltpu.VMEM((2, n_col, 128), i32),
            pltpu.SMEM((2, n_col, 128), i32),
            pltpu.VMEM((2 * rows, width), f32),
            pltpu.VMEM((2, stored, orb, orb), f32),
            pltpu.VMEM((2, orb, orb), f32),
            pltpu.VMEM((2, stored // 2, orb, width), f32),
            pltpu.VMEM((2, 2, up(rows, 128), up(cols, 128)), f32),
            down, down, down, down, upward, upward, upward, upward,
            pltpu.VMEM((DEGREE, cols, width), f32),
            pltpu.VMEM((DEGREE, rows, width), f32),
            pltpu.VMEM((2, rows, width), f32),
            pltpu.VMEM((DEGREE, rows, width), f32),
            pltpu.VMEM((DEGREE, cols, width), f32),
            pltpu.VMEM((DEGREE, half - 1, orb, width), f32),
            pltpu.VMEM((DEGREE, n_row - 1, orb, width), f32),
            pltpu.SemaphoreType.DMA((6,)),
            pltpu.SemaphoreType.DMA((5, 4)),
            pltpu.SemaphoreType.DMA((5, 4)),
        ],
        compiler_params=pltpu.CompilerParams(
            collective_id=0, has_side_effects=True, vmem_limit_bytes=56 * 1024 * 1024
        ),
        cost_estimate=pl.CostEstimate(
            flops=16 * DEGREE * rows * cols * width, bytes_accessed=8 * rows * width, transcendentals=0
        ),
    )(slots, vectors, tile_data, diag_blocks[0])


def solution(mesh):
    return jax.shard_map(
        functools.partial(body, mesh.shape["row"], mesh.shape["col"]),
        mesh=mesh,
        in_specs=(
            P("row", None),
            P("row", "col", None, None, None),
            P("row", "col", None, None),
            P(("row", "col"), None, None),
        ),
        out_specs=P("row", None),
        check_vma=False,
    )
```

```python
import functools

import jax
import jax.numpy as jnp
from jax import lax
from jax.experimental import pallas as pl
from jax.experimental.pallas import tpu as pltpu
from jax.sharding import PartitionSpec as P

DEGREE = 3
MESH = pl.DeviceIdType.MESH

filter_low = 0.0
filter_high = 8.0


def halves(value):
    high = value.astype(jnp.bfloat16)
    return high, (value - high.astype(jnp.float32)).astype(jnp.bfloat16)


def product(left_high, left_low, right):
    right_high, right_low = halves(right)
    dot = functools.partial(jnp.dot, preferred_element_type=jnp.float32)
    return dot(left_high, right_high) + (dot(left_high, right_low) + dot(left_low, right_high))


def mix(high, low, field, left):
    far = pltpu.roll(field, field.shape[1] // 2, 1)
    both = product(high[0], low[0], field) + product(high[1], low[1], far)
    count = both.shape[0] // 2
    return jnp.where(left, both[:count], both[count:])


def kernel(
    n_row, n_col, pos_hbm, vectors_hbm, tiles_hbm, diag_hbm, out_ref,
    pos, slots, slots_smem, vectors, tiles, diags, packed, dense,
    down_h, down_l, up_h, up_l,
    col_field, row_field, final, direct, mirror, direct_in, mirror_in,
    load_sem, send_sem, recv_sem,
):
    orb = diag_hbm.shape[0]
    width = vectors.shape[1]
    stored = tiles.shape[1]
    half = n_col // 2
    rows, cols = half * orb, n_row * orb
    r, c = lax.axis_index("row"), lax.axis_index("col")
    h, m = c // half, c % half
    other = 1 - h
    partner = other * half + m
    row_peers = [lax.rem(r + d, n_row) for d in range(1, n_row)]
    col_slots = [lax.rem(m + d, half) for d in range(1, half)]
    left = lax.broadcasted_iota(jnp.int32, (1, width), 1) < width // 2

    def block(index):
        return pl.ds(pl.multiple_of(index * orb, 8), orb)

    loads = [
        pltpu.make_async_copy(pos_hbm, pos, load_sem.at[0]),
        pltpu.make_async_copy(vectors_hbm, vectors, load_sem.at[1]),
        pltpu.make_async_copy(tiles_hbm, tiles.at[0], load_sem.at[2]),
        pltpu.make_async_copy(diag_hbm, diags.at[0], load_sem.at[3]),
    ]
    for load in loads:
        load.start()

    barrier = pltpu.get_barrier_semaphore()
    for peer in row_peers:
        pl.semaphore_signal(barrier, inc=1, device_id=(peer, c), device_id_type=MESH)
    for slot in col_slots:
        pl.semaphore_signal(barrier, inc=1, device_id=(r, h * half + slot), device_id_type=MESH)
    pl.semaphore_signal(barrier, inc=1, device_id=(r, partner), device_id_type=MESH)

    def copy(kind, step, source, target, device):
        return pltpu.make_async_remote_copy(
            src_ref=source, dst_ref=target,
            send_sem=send_sem.at[kind, step], recv_sem=recv_sem.at[kind, step],
            device_id=device, device_id_type=MESH,
        )

    def region_of(kind, step):
        if kind == 0:
            return col_field.at[step, pl.ds(0, cols - orb)]
        if kind == 1:
            return direct_in.at[step]
        if kind == 2:
            return mirror_in.at[step]
        if kind == 3:
            return row_field.at[step, pl.ds(0, rows - orb)]
        if step == 3:
            return final.at[0, pl.ds(0, rows - orb)]
        if step == 0:
            return packed.at[1]
        if step == 1:
            return slots.at[1]
        return final.at[0, pl.ds(0, orb)]

    def awaited(kind, step):
        region = region_of(kind, step)
        return copy(kind, step, region, region, (r, c))

    loads[2].wait()
    loads[3].wait()
    part = (width - 2 * orb) // 8 * 8
    for k in range(stored // 2):
        pieces = [tiles[0, 2 * k], tiles[0, 2 * k + 1]]
        if k * part < orb:
            share = min(part, orb - k * part)
            pieces.append(diags[0, :, pl.ds(k * part, share)])
            if share < part:
                pieces.append(jnp.zeros((orb, part - share), jnp.float32))
        else:
            pieces.append(jnp.zeros((orb, part), jnp.float32))
        packed[0, k] = jnp.concatenate(pieces, axis=1)
    loads[0].wait()
    at_row = lax.broadcasted_iota(jnp.int32, (n_col, 128), 0)
    at_col = lax.broadcasted_iota(jnp.int32, (n_col, 128), 1)
    table = jnp.zeros((n_col, 128), jnp.int32)
    for t in range(stored):
        table = jnp.where((at_row == pos[0, t]) & (at_col == pos[1, t]), t + 1, table)
    slots[0] = table
    own_slots = pltpu.make_async_copy(slots.at[0], slots_smem.at[0], load_sem.at[4])
    own_slots.start()
    loads[1].wait()
    top, bottom = vectors[pl.ds(0, rows), :], vectors[pl.ds(rows, rows), :]
    first = jnp.where(h == 0, top, pltpu.roll(top, width // 2, 1))
    second = jnp.where(h == 0, pltpu.roll(bottom, width // 2, 1), bottom)
    row_field[0] = jnp.where(left, first, second)
    own = row_field[0, block(m), :]
    col_field[0, block(r), :] = own

    pl.semaphore_wait(barrier, n_row + half - 1)

    copy(4, 1, slots.at[0], slots.at[1], (r, partner)).start()
    copy(4, 0, packed.at[0], packed.at[1], (r, partner)).start()
    for peer in row_peers:
        copy(0, 0, row_field.at[0, block(m)], col_field.at[0, block(r)], (peer, c)).start()

    dense[...] = jnp.zeros_like(dense)
    own_slots.wait()

    def fill(source, place):
        for a in range(2):
            def one(i, carry):
                parts = []
                for j in range(n_row):
                    slot = slots_smem[source, a * half + i, j]
                    tile = tiles[source, jnp.maximum(slot - 1, 0)]
                    parts.append(jnp.where(slot > 0, tile, 0.0))
                dense[a, block(i), pl.ds(0, cols)] = jnp.concatenate(parts, axis=1)
                return carry

            lax.fori_loop(0, half, one, 0)
            turned = place if a == 0 else 1 - place
            panel = dense[a]
            there = pl.ds(a * rows, rows)
            down_h[turned, there, :], down_l[turned, there, :] = halves(panel[:rows, :cols])
            there = pl.ds(pl.multiple_of(place * cols, 16), cols)
            up_h[turned, there, :], up_l[turned, there, :] = halves(panel.T[:cols, :rows])

    fill(0, h)
    awaited(4, 1).wait_recv()
    other_slots = pltpu.make_async_copy(slots.at[1], slots_smem.at[1], load_sem.at[5])
    other_slots.start()
    other_slots.wait()
    awaited(4, 0).wait_recv()
    pieces = []
    for k in range(stored // 2):
        pair = packed[1, k]
        tiles[1, 2 * k] = pair[:, :orb]
        tiles[1, 2 * k + 1] = pair[:, orb : 2 * orb]
        if k * part < orb:
            pieces.append(pair[:, 2 * orb : 2 * orb + min(part, orb - k * part)])
    diags[1] = jnp.concatenate(pieces, axis=1)
    fill(1, other)

    diag_left = halves(jnp.where(h == 0, diags[0], diags[1]))
    diag_right = halves(jnp.where(h == 0, diags[1], diags[0]))

    centre = 0.5 * (filter_high + filter_low)
    half_width = 0.5 * (filter_high - filter_low)

    def one_step(step, carry):
        previous, own = carry
        awaited(0, step).wait_recv()
        direct[step] = mix(down_h, down_l, col_field[step], left)
        for d, slot in enumerate(col_slots):
            copy(1, step, direct.at[step, block(slot)], direct_in.at[step, d], (r, h * half + slot)).start()

        @pl.when(step > 0)
        def _():
            awaited(3, step).wait_recv()

        mirror[step] = mix(up_h, up_l, row_field[step], left)
        for d, peer in enumerate(row_peers):
            copy(2, step, mirror.at[step, block(peer)], mirror_in.at[step, d], (peer, c)).start()
        image = jnp.where(left, product(*diag_left, own), product(*diag_right, own))
        image = image + direct[step, block(m), :] + mirror[step, block(r), :]
        awaited(1, step).wait_recv()
        for d in range(half - 1):
            image = image + direct_in[step, d]
        awaited(2, step).wait_recv()
        for d in range(n_row - 1):
            image = image + mirror_in[step, d]
        shifted = (image - centre * own) / half_width
        following = jnp.where(step == 0, shifted, 2.0 * shifted - previous)

        @pl.when(step < DEGREE - 1)
        def _():
            row_field[step + 1, block(m), :] = following
            col_field[step + 1, block(r), :] = following
            mine = row_field.at[step + 1, block(m)]
            for peer in row_peers:
                copy(0, step + 1, mine, col_field.at[step + 1, block(r)], (peer, c)).start()
            for slot in col_slots:
                copy(3, step + 1, mine, mine, (r, h * half + slot)).start()

        return own, following

    _, own = lax.fori_loop(0, DEGREE, one_step, (jnp.zeros_like(own), own))
    final[h, block(m), :] = own
    mine, theirs = final.at[h, block(m)], final.at[other, block(m)]
    copy(4, 2, mine, mine, (r, partner)).start()
    for slot in col_slots:
        copy(3, 0, mine, mine, (r, h * half + slot)).start()
    awaited(4, 2).wait_recv()
    for slot in col_slots:
        copy(4, 3, theirs, theirs, (r, h * half + slot)).start()
    awaited(3, 0).wait_recv()
    awaited(4, 3).wait_recv()
    low, high = final[0], final[1]
    out_ref[pl.ds(0, rows), :] = jnp.where(left, low, pltpu.roll(high, width // 2, 1))
    out_ref[pl.ds(rows, rows), :] = jnp.where(left, pltpu.roll(low, width // 2, 1), high)
    for kind in range(5):
        for step in range(4 if kind == 4 else DEGREE):
            awaited(kind, step).wait_send()


def up(value, unit):
    return (value + unit - 1) // unit * unit


def body(n_row, n_col, vectors, tiles, tile_pos, diag_blocks):
    tile_data = tiles[0, 0]
    stored, orb, _ = tile_data.shape
    width = vectors.shape[1]
    half = n_col // 2
    rows, cols = half * orb, n_row * orb
    hbm = pl.BlockSpec(memory_space=pl.ANY)
    f32, bf16, i32 = jnp.float32, jnp.bfloat16, jnp.int32
    down = pltpu.VMEM((2, 2 * rows, cols), bf16)
    upward = pltpu.VMEM((2, 2 * cols, rows), bf16)
    return pl.pallas_call(
        functools.partial(kernel, n_row, n_col),
        out_shape=jax.ShapeDtypeStruct((2 * rows, width), f32),
        in_specs=[hbm, hbm, hbm, hbm],
        out_specs=pl.BlockSpec(memory_space=pltpu.VMEM),
        scratch_shapes=[
            pltpu.SMEM(tile_pos.shape[2:], i32),
            pltpu.VMEM((2, n_col, 128), i32),
            pltpu.SMEM((2, n_col, 128), i32),
            pltpu.VMEM((2 * rows, width), f32),
            pltpu.VMEM((2, stored, orb, orb), f32),
            pltpu.VMEM((2, orb, orb), f32),
            pltpu.VMEM((2, stored // 2, orb, width), f32),
            pltpu.VMEM((2, up(rows, 128), up(cols, 128)), f32),
            down, down, upward, upward,
            pltpu.VMEM((DEGREE, cols, width), f32),
            pltpu.VMEM((DEGREE, rows, width), f32),
            pltpu.VMEM((2, rows, width), f32),
            pltpu.VMEM((DEGREE, rows, width), f32),
            pltpu.VMEM((DEGREE, cols, width), f32),
            pltpu.VMEM((DEGREE, half - 1, orb, width), f32),
            pltpu.VMEM((DEGREE, n_row - 1, orb, width), f32),
            pltpu.SemaphoreType.DMA((6,)),
            pltpu.SemaphoreType.DMA((5, 4)),
            pltpu.SemaphoreType.DMA((5, 4)),
        ],
        compiler_params=pltpu.CompilerParams(
            collective_id=0, has_side_effects=True, vmem_limit_bytes=56 * 1024 * 1024
        ),
        cost_estimate=pl.CostEstimate(
            flops=16 * DEGREE * rows * cols * width, bytes_accessed=8 * rows * width, transcendentals=0
        ),
    )(tile_pos[0, 0], vectors, tile_data, diag_blocks[0])


def solution(mesh):
    return jax.shard_map(
        functools.partial(body, mesh.shape["row"], mesh.shape["col"]),
        mesh=mesh,
        in_specs=(
            P("row", None),
            P("row", "col", None, None, None),
            P("row", "col", None, None),
            P(("row", "col"), None, None),
        ),
        out_specs=P("row", None),
        check_vma=False,
    )
```

```python
import functools

import jax
import jax.numpy as jnp
from jax import lax
from jax.experimental import pallas as pl
from jax.experimental.pallas import tpu as pltpu
from jax.sharding import PartitionSpec as P

DEGREE = 3
MESH = pl.DeviceIdType.MESH

filter_low = 0.0
filter_high = 8.0


def halves(value):
    high = value.astype(jnp.bfloat16)
    return high, (value - high.astype(jnp.float32)).astype(jnp.bfloat16)


def product(left_high, left_low, right):
    right_high, right_low = halves(right)
    dot = functools.partial(jnp.dot, preferred_element_type=jnp.float32)
    return dot(left_high, right_high) + (dot(left_high, right_low) + dot(left_low, right_high))


def mix(panels, field, left):
    far = pltpu.roll(field, field.shape[1] // 2, 1)
    depth = panels.shape[1] // 4
    empty = jnp.zeros((depth - field.shape[0], field.shape[1]), jnp.float32)
    pieces = [field, far] if depth == field.shape[0] else [field, empty, far, empty]
    high, low = halves(jnp.concatenate(pieces, axis=0))
    dot = functools.partial(jnp.dot, preferred_element_type=jnp.float32)
    both = dot(panels[...], jnp.concatenate([high, high], axis=0)) + dot(panels[:, pl.ds(0, 2 * depth)], low)
    count = both.shape[0] // 2
    return jnp.where(left, both[:count], both[count:])


def kernel(
    n_row, n_col, pos_hbm, vectors_hbm, tiles_hbm, diag_hbm, out_ref,
    pos, slots, slots_smem, vectors, tiles, diags, packed, dense,
    down, upward,
    col_field, row_field, final, direct, mirror, direct_in, mirror_in,
    load_sem, send_sem, recv_sem,
):
    orb = diag_hbm.shape[0]
    width = vectors.shape[1]
    stored = tiles.shape[1]
    half = n_col // 2
    rows, cols = half * orb, n_row * orb
    r, c = lax.axis_index("row"), lax.axis_index("col")
    h, m = c // half, c % half
    other = 1 - h
    partner = other * half + m
    row_peers = [lax.rem(r + d, n_row) for d in range(1, n_row)]
    col_slots = [lax.rem(m + d, half) for d in range(1, half)]
    left = lax.broadcasted_iota(jnp.int32, (1, width), 1) < width // 2

    def block(index):
        return pl.ds(pl.multiple_of(index * orb, 8), orb)

    loads = [
        pltpu.make_async_copy(pos_hbm, pos, load_sem.at[0]),
        pltpu.make_async_copy(vectors_hbm, vectors, load_sem.at[1]),
        pltpu.make_async_copy(tiles_hbm, tiles.at[0], load_sem.at[2]),
        pltpu.make_async_copy(diag_hbm, diags.at[0], load_sem.at[3]),
    ]
    for load in loads:
        load.start()

    barrier = pltpu.get_barrier_semaphore()
    for peer in row_peers:
        pl.semaphore_signal(barrier, inc=1, device_id=(peer, c), device_id_type=MESH)
    for slot in col_slots:
        pl.semaphore_signal(barrier, inc=1, device_id=(r, h * half + slot), device_id_type=MESH)
    pl.semaphore_signal(barrier, inc=1, device_id=(r, partner), device_id_type=MESH)

    def copy(kind, step, source, target, device):
        return pltpu.make_async_remote_copy(
            src_ref=source, dst_ref=target,
            send_sem=send_sem.at[kind, step], recv_sem=recv_sem.at[kind, step],
            device_id=device, device_id_type=MESH,
        )

    def region_of(kind, step):
        if kind == 0:
            return col_field.at[step, pl.ds(0, cols - orb)]
        if kind == 1:
            return direct_in.at[step]
        if kind == 2:
            return mirror_in.at[step]
        if kind == 3:
            return row_field.at[step, pl.ds(0, rows - orb)]
        if step == 3:
            return final.at[0, pl.ds(0, rows - orb)]
        if step == 0:
            return packed.at[1]
        if step == 1:
            return slots.at[1]
        return final.at[0, pl.ds(0, orb)]

    def awaited(kind, step):
        region = region_of(kind, step)
        return copy(kind, step, region, region, (r, c))

    loads[2].wait()
    loads[3].wait()
    part = (width - 2 * orb) // 8 * 8
    for k in range(stored // 2):
        pieces = [tiles[0, 2 * k], tiles[0, 2 * k + 1]]
        if k * part < orb:
            share = min(part, orb - k * part)
            pieces.append(diags[0, :, pl.ds(k * part, share)])
            if share < part:
                pieces.append(jnp.zeros((orb, part - share), jnp.float32))
        else:
            pieces.append(jnp.zeros((orb, part), jnp.float32))
        packed[0, k] = jnp.concatenate(pieces, axis=1)
    loads[0].wait()
    at_row = lax.broadcasted_iota(jnp.int32, (n_col, 128), 0)
    at_col = lax.broadcasted_iota(jnp.int32, (n_col, 128), 1)
    table = jnp.zeros((n_col, 128), jnp.int32)
    for t in range(stored):
        table = jnp.where((at_row == pos[0, t]) & (at_col == pos[1, t]), t + 1, table)
    slots[0] = table
    own_slots = pltpu.make_async_copy(slots.at[0], slots_smem.at[0], load_sem.at[4])
    own_slots.start()
    loads[1].wait()
    top, bottom = vectors[pl.ds(0, rows), :], vectors[pl.ds(rows, rows), :]
    first = jnp.where(h == 0, top, pltpu.roll(top, width // 2, 1))
    second = jnp.where(h == 0, pltpu.roll(bottom, width // 2, 1), bottom)
    row_field[0] = jnp.where(left, first, second)
    own = row_field[0, block(m), :]
    col_field[0, block(r), :] = own

    pl.semaphore_wait(barrier, n_row + half - 1)

    copy(4, 1, slots.at[0], slots.at[1], (r, partner)).start()
    copy(4, 0, packed.at[0], packed.at[1], (r, partner)).start()
    for peer in row_peers:
        copy(0, 0, row_field.at[0, block(m)], col_field.at[0, block(r)], (peer, c)).start()

    dense[...] = jnp.zeros_like(dense)
    own_slots.wait()

    def fill(source, place):
        for a in range(2):
            def one(i, carry):
                parts = []
                for j in range(n_row):
                    slot = slots_smem[source, a * half + i, j]
                    tile = tiles[source, jnp.maximum(slot - 1, 0)]
                    parts.append(jnp.where(slot > 0, tile, 0.0))
                dense[a, block(i), pl.ds(0, cols)] = jnp.concatenate(parts, axis=1)
                return carry

            lax.fori_loop(0, half, one, 0)
            put(down, place if a == 0 else 1 - place, pl.ds(a * rows, rows), dense[a, pl.ds(0, rows), :])

    def put(panels, turned, there, panel):
        depth = panel.shape[1]
        high, low = halves(panel)
        panels[there, pl.ds(pl.multiple_of(turned * depth, 128), depth)] = high
        panels[there, pl.ds(pl.multiple_of((turned + 2) * depth, 128), depth)] = low

    def turn(place):
        there = pl.ds(pl.multiple_of(place * cols, 16), cols)
        for a in range(2):
            put(upward, place if a == 0 else 1 - place, there, dense[a].T[:cols])

    fill(0, h)
    turn(h)
    awaited(4, 1).wait_recv()
    other_slots = pltpu.make_async_copy(slots.at[1], slots_smem.at[1], load_sem.at[5])
    other_slots.start()
    other_slots.wait()
    awaited(4, 0).wait_recv()
    pieces = []
    for k in range(stored // 2):
        pair = packed[1, k]
        tiles[1, 2 * k] = pair[:, :orb]
        tiles[1, 2 * k + 1] = pair[:, orb : 2 * orb]
        if k * part < orb:
            pieces.append(pair[:, 2 * orb : 2 * orb + min(part, orb - k * part)])
    diags[1] = jnp.concatenate(pieces, axis=1)
    fill(1, other)

    diag_left = halves(jnp.where(h == 0, diags[0], diags[1]))
    diag_right = halves(jnp.where(h == 0, diags[1], diags[0]))

    centre = 0.5 * (filter_high + filter_low)
    half_width = 0.5 * (filter_high - filter_low)

    def one_step(step, carry):
        previous, own = carry
        awaited(0, step).wait_recv()
        direct[step] = mix(down, col_field[step], left)
        for d, slot in enumerate(col_slots):
            copy(1, step, direct.at[step, block(slot)], direct_in.at[step, d], (r, h * half + slot)).start()

        @pl.when(step == 0)
        def _():
            turn(other)

        @pl.when(step > 0)
        def _():
            awaited(3, step).wait_recv()

        mirror[step] = mix(upward, row_field[step], left)
        for d, peer in enumerate(row_peers):
            copy(2, step, mirror.at[step, block(peer)], mirror_in.at[step, d], (peer, c)).start()
        image = jnp.where(left, product(*diag_left, own), product(*diag_right, own))
        image = image + direct[step, block(m), :] + mirror[step, block(r), :]
        awaited(1, step).wait_recv()
        for d in range(half - 1):
            image = image + direct_in[step, d]
        awaited(2, step).wait_recv()
        for d in range(n_row - 1):
            image = image + mirror_in[step, d]
        shifted = (image - centre * own) / half_width
        following = jnp.where(step == 0, shifted, 2.0 * shifted - previous)

        @pl.when(step < DEGREE - 1)
        def _():
            row_field[step + 1, block(m), :] = following
            col_field[step + 1, block(r), :] = following
            mine = row_field.at[step + 1, block(m)]
            for peer in row_peers:
                copy(0, step + 1, mine, col_field.at[step + 1, block(r)], (peer, c)).start()
            for slot in col_slots:
                copy(3, step + 1, mine, mine, (r, h * half + slot)).start()

        return own, following

    _, own = lax.fori_loop(0, DEGREE, one_step, (jnp.zeros_like(own), own))
    final[h, block(m), :] = own
    mine, theirs = final.at[h, block(m)], final.at[other, block(m)]
    copy(4, 2, mine, mine, (r, partner)).start()
    for slot in col_slots:
        copy(3, 0, mine, mine, (r, h * half + slot)).start()
    awaited(4, 2).wait_recv()
    for slot in col_slots:
        copy(4, 3, theirs, theirs, (r, h * half + slot)).start()
    awaited(3, 0).wait_recv()
    awaited(4, 3).wait_recv()
    low, high = final[0], final[1]
    out_ref[pl.ds(0, rows), :] = jnp.where(left, low, pltpu.roll(high, width // 2, 1))
    out_ref[pl.ds(rows, rows), :] = jnp.where(left, pltpu.roll(low, width // 2, 1), high)
    for kind in range(5):
        for step in range(4 if kind == 4 else DEGREE):
            awaited(kind, step).wait_send()


def up(value, unit):
    return (value + unit - 1) // unit * unit


def body(n_row, n_col, vectors, tiles, tile_pos, diag_blocks):
    tile_data = tiles[0, 0]
    stored, orb, _ = tile_data.shape
    width = vectors.shape[1]
    half = n_col // 2
    rows, cols = half * orb, n_row * orb
    hbm = pl.BlockSpec(memory_space=pl.ANY)
    f32, bf16, i32 = jnp.float32, jnp.bfloat16, jnp.int32
    tall, broad = up(rows, 128), up(cols, 128)
    return pl.pallas_call(
        functools.partial(kernel, n_row, n_col),
        out_shape=jax.ShapeDtypeStruct((2 * rows, width), f32),
        in_specs=[hbm, hbm, hbm, hbm],
        out_specs=pl.BlockSpec(memory_space=pltpu.VMEM),
        scratch_shapes=[
            pltpu.SMEM(tile_pos.shape[2:], i32),
            pltpu.VMEM((2, n_col, 128), i32),
            pltpu.SMEM((2, n_col, 128), i32),
            pltpu.VMEM((2 * rows, width), f32),
            pltpu.VMEM((2, stored, orb, orb), f32),
            pltpu.VMEM((2, orb, orb), f32),
            pltpu.VMEM((2, stored // 2, orb, width), f32),
            pltpu.VMEM((2, tall, broad), f32),
            pltpu.VMEM((2 * rows, 4 * broad), bf16),
            pltpu.VMEM((2 * cols, 4 * tall), bf16),
            pltpu.VMEM((DEGREE, cols, width), f32),
            pltpu.VMEM((DEGREE, rows, width), f32),
            pltpu.VMEM((2, rows, width), f32),
            pltpu.VMEM((DEGREE, rows, width), f32),
            pltpu.VMEM((DEGREE, cols, width), f32),
            pltpu.VMEM((DEGREE, half - 1, orb, width), f32),
            pltpu.VMEM((DEGREE, n_row - 1, orb, width), f32),
            pltpu.SemaphoreType.DMA((6,)),
            pltpu.SemaphoreType.DMA((5, 4)),
            pltpu.SemaphoreType.DMA((5, 4)),
        ],
        compiler_params=pltpu.CompilerParams(
            collective_id=0, has_side_effects=True, vmem_limit_bytes=56 * 1024 * 1024
        ),
        cost_estimate=pl.CostEstimate(
            flops=16 * DEGREE * rows * cols * width, bytes_accessed=8 * rows * width, transcendentals=0
        ),
    )(tile_pos[0, 0], vectors, tile_data, diag_blocks[0])


def solution(mesh):
    return jax.shard_map(
        functools.partial(body, mesh.shape["row"], mesh.shape["col"]),
        mesh=mesh,
        in_specs=(
            P("row", None),
            P("row", "col", None, None, None),
            P("row", "col", None, None),
            P(("row", "col"), None, None),
        ),
        out_specs=P("row", None),
        check_vma=False,
    )
```

```python
import functools

import jax
import jax.numpy as jnp
from jax import lax
from jax.experimental import pallas as pl
from jax.experimental.pallas import tpu as pltpu
from jax.sharding import PartitionSpec as P

DEGREE = 3
MESH = pl.DeviceIdType.MESH

filter_low = 0.0
filter_high = 8.0


def halves(value):
    high = value.astype(jnp.bfloat16)
    return high, (value - high.astype(jnp.float32)).astype(jnp.bfloat16)


def product(left_high, left_low, right):
    right_high, right_low = halves(right)
    dot = functools.partial(jnp.dot, preferred_element_type=jnp.float32)
    return dot(left_high, right_high) + (dot(left_high, right_low) + dot(left_low, right_high))


def flipped(index, mask, extent):
    bit = 1
    while bit < extent:
        if mask // bit % 2 == 1:
            index = index + bit * (1 - 2 * (index // bit % 2))
        bit *= 2
    return index


def mix(panels, field, left):
    far = pltpu.roll(field, field.shape[1] // 2, 1)
    depth = panels.shape[1] // 4
    empty = jnp.zeros((depth - field.shape[0], field.shape[1]), jnp.float32)
    pieces = [field, far] if depth == field.shape[0] else [field, empty, far, empty]
    high, low = halves(jnp.concatenate(pieces, axis=0))
    dot = functools.partial(jnp.dot, preferred_element_type=jnp.float32)
    both = dot(panels[...], jnp.concatenate([high, high], axis=0)) + dot(panels[:, pl.ds(0, 2 * depth)], low)
    count = both.shape[0] // 2
    return jnp.where(left, both[:count], both[count:])


def kernel(
    n_row, n_col, pos_hbm, vectors_hbm, tiles_hbm, diag_hbm, out_ref,
    pos, slots, slots_smem, vectors, tiles, diags, packed, dense,
    down, upward,
    col_field, row_field, final, direct, mirror, direct_in, mirror_in,
    load_sem, send_sem, recv_sem,
):
    orb = diag_hbm.shape[0]
    width = vectors.shape[1]
    stored = tiles.shape[1]
    half = n_col // 2
    rows, cols = half * orb, n_row * orb
    r, c = lax.axis_index("row"), lax.axis_index("col")
    h, m = c // half, c % half
    other = 1 - h
    partner = other * half + m
    row_peers = [flipped(r, d, n_row) for d in range(n_row - 1, 0, -1)]
    col_slots = [flipped(m, d, half) for d in range(half - 1, 0, -1)]
    left = lax.broadcasted_iota(jnp.int32, (1, width), 1) < width // 2

    def block(index):
        return pl.ds(pl.multiple_of(index * orb, 8), orb)

    loads = [
        pltpu.make_async_copy(pos_hbm, pos, load_sem.at[0]),
        pltpu.make_async_copy(vectors_hbm, vectors, load_sem.at[1]),
        pltpu.make_async_copy(tiles_hbm, tiles.at[0], load_sem.at[2]),
        pltpu.make_async_copy(diag_hbm, diags.at[0], load_sem.at[3]),
    ]
    for load in loads:
        load.start()

    barrier = pltpu.get_barrier_semaphore()
    for peer in row_peers:
        pl.semaphore_signal(barrier, inc=1, device_id=(peer, c), device_id_type=MESH)
    for slot in col_slots:
        pl.semaphore_signal(barrier, inc=1, device_id=(r, h * half + slot), device_id_type=MESH)
    pl.semaphore_signal(barrier, inc=1, device_id=(r, partner), device_id_type=MESH)

    def copy(kind, step, source, target, device):
        return pltpu.make_async_remote_copy(
            src_ref=source, dst_ref=target,
            send_sem=send_sem.at[kind, step], recv_sem=recv_sem.at[kind, step],
            device_id=device, device_id_type=MESH,
        )

    def region_of(kind, step):
        if kind == 0:
            return col_field.at[step, pl.ds(0, cols - orb)]
        if kind == 1:
            return direct_in.at[step]
        if kind == 2:
            return mirror_in.at[step]
        if kind == 3:
            return row_field.at[step, pl.ds(0, rows - orb)]
        if step == 3:
            return final.at[0, pl.ds(0, rows - orb)]
        if step == 0:
            return packed.at[1]
        if step == 1:
            return slots.at[1]
        return final.at[0, pl.ds(0, orb)]

    def awaited(kind, step):
        region = region_of(kind, step)
        return copy(kind, step, region, region, (r, c))

    loads[2].wait()
    loads[3].wait()
    part = (width - 2 * orb) // 8 * 8
    for k in range(stored // 2):
        pieces = [tiles[0, 2 * k], tiles[0, 2 * k + 1]]
        if k * part < orb:
            share = min(part, orb - k * part)
            pieces.append(diags[0, :, pl.ds(k * part, share)])
            if share < part:
                pieces.append(jnp.zeros((orb, part - share), jnp.float32))
        else:
            pieces.append(jnp.zeros((orb, part), jnp.float32))
        packed[0, k] = jnp.concatenate(pieces, axis=1)
    pl.semaphore_wait(barrier, n_row + half - 1)
    copy(4, 0, packed.at[0], packed.at[1], (r, partner)).start()
    loads[0].wait()
    at_row = lax.broadcasted_iota(jnp.int32, (n_col, 128), 0)
    at_col = lax.broadcasted_iota(jnp.int32, (n_col, 128), 1)
    table = jnp.zeros((n_col, 128), jnp.int32)
    for t in range(stored):
        table = jnp.where((at_row == pos[0, t]) & (at_col == pos[1, t]), t + 1, table)
    slots[0] = table
    own_slots = pltpu.make_async_copy(slots.at[0], slots_smem.at[0], load_sem.at[4])
    own_slots.start()
    loads[1].wait()
    top, bottom = vectors[pl.ds(0, rows), :], vectors[pl.ds(rows, rows), :]
    first = jnp.where(h == 0, top, pltpu.roll(top, width // 2, 1))
    second = jnp.where(h == 0, pltpu.roll(bottom, width // 2, 1), bottom)
    row_field[0] = jnp.where(left, first, second)
    own = row_field[0, block(m), :]
    col_field[0, block(r), :] = own

    copy(4, 1, slots.at[0], slots.at[1], (r, partner)).start()
    for peer in row_peers:
        copy(0, 0, row_field.at[0, block(m)], col_field.at[0, block(r)], (peer, c)).start()

    dense[...] = jnp.zeros_like(dense)
    own_slots.wait()

    def fill(source, place):
        for a in range(2):
            def one(i, carry):
                parts = []
                for j in range(n_row):
                    slot = slots_smem[source, a * half + i, j]
                    tile = tiles[source, jnp.maximum(slot - 1, 0)]
                    parts.append(jnp.where(slot > 0, tile, 0.0))
                dense[a, block(i), pl.ds(0, cols)] = jnp.concatenate(parts, axis=1)
                return carry

            lax.fori_loop(0, half, one, 0)
            put(down, place if a == 0 else 1 - place, pl.ds(a * rows, rows), dense[a, pl.ds(0, rows), :])

    def put(panels, turned, there, panel):
        depth = panel.shape[1]
        high, low = halves(panel)
        panels[there, pl.ds(pl.multiple_of(turned * depth, 128), depth)] = high
        panels[there, pl.ds(pl.multiple_of((turned + 2) * depth, 128), depth)] = low

    def turn(place):
        there = pl.ds(pl.multiple_of(place * cols, 16), cols)
        for a in range(2):
            put(upward, place if a == 0 else 1 - place, there, dense[a].T[:cols])

    fill(0, h)
    turn(h)
    awaited(4, 1).wait_recv()
    other_slots = pltpu.make_async_copy(slots.at[1], slots_smem.at[1], load_sem.at[5])
    other_slots.start()
    other_slots.wait()
    awaited(4, 0).wait_recv()
    pieces = []
    for k in range(stored // 2):
        pair = packed[1, k]
        tiles[1, 2 * k] = pair[:, :orb]
        tiles[1, 2 * k + 1] = pair[:, orb : 2 * orb]
        if k * part < orb:
            pieces.append(pair[:, 2 * orb : 2 * orb + min(part, orb - k * part)])
    diags[1] = jnp.concatenate(pieces, axis=1)
    fill(1, other)

    diag_left = halves(jnp.where(h == 0, diags[0], diags[1]))
    diag_right = halves(jnp.where(h == 0, diags[1], diags[0]))

    centre = 0.5 * (filter_high + filter_low)
    half_width = 0.5 * (filter_high - filter_low)

    def one_step(step, carry):
        previous, own = carry
        awaited(0, step).wait_recv()
        direct[step] = mix(down, col_field[step], left)
        for d, slot in enumerate(col_slots):
            copy(1, step, direct.at[step, block(slot)], direct_in.at[step, d], (r, h * half + slot)).start()

        @pl.when(step == 0)
        def _():
            turn(other)

        @pl.when(step > 0)
        def _():
            awaited(3, step).wait_recv()

        mirror[step] = mix(upward, row_field[step], left)
        for d, peer in enumerate(row_peers):
            copy(2, step, mirror.at[step, block(peer)], mirror_in.at[step, d], (peer, c)).start()
        image = jnp.where(left, product(*diag_left, own), product(*diag_right, own))
        image = image + direct[step, block(m), :] + mirror[step, block(r), :]
        awaited(1, step).wait_recv()
        for d in range(half - 1):
            image = image + direct_in[step, d]
        awaited(2, step).wait_recv()
        for d in range(n_row - 1):
            image = image + mirror_in[step, d]
        shifted = (image - centre * own) / half_width
        following = jnp.where(step == 0, shifted, 2.0 * shifted - previous)

        @pl.when(step < DEGREE - 1)
        def _():
            row_field[step + 1, block(m), :] = following
            col_field[step + 1, block(r), :] = following
            mine = row_field.at[step + 1, block(m)]
            for peer in row_peers:
                copy(0, step + 1, mine, col_field.at[step + 1, block(r)], (peer, c)).start()
            for slot in col_slots:
                copy(3, step + 1, mine, mine, (r, h * half + slot)).start()

        return own, following

    _, own = lax.fori_loop(0, DEGREE, one_step, (jnp.zeros_like(own), own))
    final[h, block(m), :] = own
    mine, theirs = final.at[h, block(m)], final.at[other, block(m)]
    copy(4, 2, mine, mine, (r, partner)).start()
    for slot in col_slots:
        copy(3, 0, mine, mine, (r, h * half + slot)).start()
    awaited(4, 2).wait_recv()
    for slot in col_slots:
        copy(4, 3, theirs, theirs, (r, h * half + slot)).start()
    awaited(3, 0).wait_recv()
    awaited(4, 3).wait_recv()
    low, high = final[0], final[1]
    out_ref[pl.ds(0, rows), :] = jnp.where(left, low, pltpu.roll(high, width // 2, 1))
    out_ref[pl.ds(rows, rows), :] = jnp.where(left, pltpu.roll(low, width // 2, 1), high)
    for kind in range(5):
        for step in range(4 if kind == 4 else DEGREE):
            awaited(kind, step).wait_send()


def up(value, unit):
    return (value + unit - 1) // unit * unit


def body(n_row, n_col, vectors, tiles, tile_pos, diag_blocks):
    tile_data = tiles[0, 0]
    stored, orb, _ = tile_data.shape
    width = vectors.shape[1]
    half = n_col // 2
    rows, cols = half * orb, n_row * orb
    hbm = pl.BlockSpec(memory_space=pl.ANY)
    f32, bf16, i32 = jnp.float32, jnp.bfloat16, jnp.int32
    tall, broad = up(rows, 128), up(cols, 128)
    return pl.pallas_call(
        functools.partial(kernel, n_row, n_col),
        out_shape=jax.ShapeDtypeStruct((2 * rows, width), f32),
        in_specs=[hbm, hbm, hbm, hbm],
        out_specs=pl.BlockSpec(memory_space=pltpu.VMEM),
        scratch_shapes=[
            pltpu.SMEM(tile_pos.shape[2:], i32),
            pltpu.VMEM((2, n_col, 128), i32),
            pltpu.SMEM((2, n_col, 128), i32),
            pltpu.VMEM((2 * rows, width), f32),
            pltpu.VMEM((2, stored, orb, orb), f32),
            pltpu.VMEM((2, orb, orb), f32),
            pltpu.VMEM((2, stored // 2, orb, width), f32),
            pltpu.VMEM((2, tall, broad), f32),
            pltpu.VMEM((2 * rows, 4 * broad), bf16),
            pltpu.VMEM((2 * cols, 4 * tall), bf16),
            pltpu.VMEM((DEGREE, cols, width), f32),
            pltpu.VMEM((DEGREE, rows, width), f32),
            pltpu.VMEM((2, rows, width), f32),
            pltpu.VMEM((DEGREE, rows, width), f32),
            pltpu.VMEM((DEGREE, cols, width), f32),
            pltpu.VMEM((DEGREE, half - 1, orb, width), f32),
            pltpu.VMEM((DEGREE, n_row - 1, orb, width), f32),
            pltpu.SemaphoreType.DMA((6,)),
            pltpu.SemaphoreType.DMA((5, 4)),
            pltpu.SemaphoreType.DMA((5, 4)),
        ],
        compiler_params=pltpu.CompilerParams(
            collective_id=0, has_side_effects=True, vmem_limit_bytes=54912 * 1024
        ),
        cost_estimate=pl.CostEstimate(
            flops=16 * DEGREE * rows * cols * width, bytes_accessed=8 * rows * width, transcendentals=0
        ),
    )(tile_pos[0, 0], vectors, tile_data, diag_blocks[0])


def solution(mesh):
    return jax.shard_map(
        functools.partial(body, mesh.shape["row"], mesh.shape["col"]),
        mesh=mesh,
        in_specs=(
            P("row", None),
            P("row", "col", None, None, None),
            P("row", "col", None, None),
            P(("row", "col"), None, None),
        ),
        out_specs=P("row", None),
        check_vma=False,
    )
```

```python
import functools

import jax
import jax.numpy as jnp
from jax import lax
from jax.experimental import pallas as pl
from jax.experimental.pallas import tpu as pltpu
from jax.sharding import PartitionSpec as P

DEGREE = 3
MESH = pl.DeviceIdType.MESH

filter_low = 0.0
filter_high = 8.0


def halves(value):
    high = value.astype(jnp.bfloat16)
    return high, (value - high.astype(jnp.float32)).astype(jnp.bfloat16)


def product(left_high, left_low, right):
    right_high, right_low = halves(right)
    dot = functools.partial(jnp.dot, preferred_element_type=jnp.float32)
    return dot(left_high, right_high) + (dot(left_high, right_low) + dot(left_low, right_high))


def mix(panels, field, left):
    far = pltpu.roll(field, field.shape[1] // 2, 1)
    depth = panels.shape[1] // 4
    empty = jnp.zeros((depth - field.shape[0], field.shape[1]), jnp.float32)
    pieces = [field, far] if depth == field.shape[0] else [field, empty, far, empty]
    high, low = halves(jnp.concatenate(pieces, axis=0))
    dot = functools.partial(jnp.dot, preferred_element_type=jnp.float32)
    both = dot(panels[...], jnp.concatenate([high, high], axis=0)) + dot(panels[:, pl.ds(0, 2 * depth)], low)
    count = both.shape[0] // 2
    return jnp.where(left, both[:count], both[count:])


def kernel(
    n_row, n_col, pos_hbm, vectors_hbm, tiles_hbm, diag_hbm, out_ref,
    pos, slots, slots_smem, vectors, tiles, diags, packed, dense,
    down, upward,
    col_field, row_field, final, direct, mirror, direct_in, mirror_in,
    load_sem, send_sem, recv_sem,
):
    orb = diag_hbm.shape[0]
    width = vectors.shape[1]
    stored = tiles.shape[1]
    half = n_col // 2
    rows, cols = half * orb, n_row * orb
    r, c = lax.axis_index("row"), lax.axis_index("col")
    h, m = c // half, c % half
    other = 1 - h
    partner = other * half + m
    row_peers = [lax.rem(r + d, n_row) for d in range(1, n_row)]
    col_slots = [lax.rem(m + d, half) for d in range(1, half)]
    left = lax.broadcasted_iota(jnp.int32, (1, width), 1) < width // 2

    def block(index):
        return pl.ds(pl.multiple_of(index * orb, 8), orb)

    loads = [
        pltpu.make_async_copy(pos_hbm, pos, load_sem.at[0]),
        pltpu.make_async_copy(vectors_hbm, vectors, load_sem.at[1]),
        pltpu.make_async_copy(tiles_hbm, tiles.at[0], load_sem.at[2]),
        pltpu.make_async_copy(diag_hbm, diags.at[0], load_sem.at[3]),
    ]
    for load in loads:
        load.start()

    barrier = pltpu.get_barrier_semaphore()
    for peer in row_peers:
        pl.semaphore_signal(barrier, inc=1, device_id=(peer, c), device_id_type=MESH)
    for slot in col_slots:
        pl.semaphore_signal(barrier, inc=1, device_id=(r, h * half + slot), device_id_type=MESH)
    pl.semaphore_signal(barrier, inc=1, device_id=(r, partner), device_id_type=MESH)

    def copy(kind, step, source, target, device):
        return pltpu.make_async_remote_copy(
            src_ref=source, dst_ref=target,
            send_sem=send_sem.at[kind, step], recv_sem=recv_sem.at[kind, step],
            device_id=device, device_id_type=MESH,
        )

    def region_of(kind, step):
        if kind == 0:
            return col_field.at[step, pl.ds(0, cols - orb)]
        if kind == 1:
            return direct_in.at[step]
        if kind == 2:
            return mirror_in.at[step]
        if kind == 3:
            return row_field.at[step, pl.ds(0, rows - orb)]
        if step == 3:
            return final.at[0, pl.ds(0, rows - orb)]
        if step == 0:
            return packed.at[1]
        if step == 1:
            return slots.at[1]
        return final.at[0, pl.ds(0, orb)]

    def awaited(kind, step):
        region = region_of(kind, step)
        return copy(kind, step, region, region, (r, c))

    loads[2].wait()
    loads[3].wait()
    part = (width - 2 * orb) // 8 * 8
    for k in range(stored // 2):
        pieces = [tiles[0, 2 * k], tiles[0, 2 * k + 1]]
        if k * part < orb:
            share = min(part, orb - k * part)
            pieces.append(diags[0, :, pl.ds(k * part, share)])
            if share < part:
                pieces.append(jnp.zeros((orb, part - share), jnp.float32))
        else:
            pieces.append(jnp.zeros((orb, part), jnp.float32))
        packed[0, k] = jnp.concatenate(pieces, axis=1)
    pl.semaphore_wait(barrier, n_row + half - 1)
    copy(4, 0, packed.at[0], packed.at[1], (r, partner)).start()
    loads[0].wait()
    at_row = lax.broadcasted_iota(jnp.int32, (n_col, 128), 0)
    at_col = lax.broadcasted_iota(jnp.int32, (n_col, 128), 1)
    table = jnp.zeros((n_col, 128), jnp.int32)
    for t in range(stored):
        table = jnp.where((at_row == pos[0, t]) & (at_col == pos[1, t]), t + 1, table)
    slots[0] = table
    own_slots = pltpu.make_async_copy(slots.at[0], slots_smem.at[0], load_sem.at[4])
    own_slots.start()
    loads[1].wait()
    top, bottom = vectors[pl.ds(0, rows), :], vectors[pl.ds(rows, rows), :]
    first = jnp.where(h == 0, top, pltpu.roll(top, width // 2, 1))
    second = jnp.where(h == 0, pltpu.roll(bottom, width // 2, 1), bottom)
    row_field[0] = jnp.where(left, first, second)
    own = row_field[0, block(m), :]
    col_field[0, block(r), :] = own

    copy(4, 1, slots.at[0], slots.at[1], (r, partner)).start()
    for peer in row_peers:
        copy(0, 0, row_field.at[0, block(m)], col_field.at[0, block(r)], (peer, c)).start()

    dense[...] = jnp.zeros_like(dense)
    own_slots.wait()

    def fill(source, place):
        for a in range(2):
            def one(i, carry):
                parts = []
                for j in range(n_row):
                    slot = slots_smem[source, a * half + i, j]
                    tile = tiles[source, jnp.maximum(slot - 1, 0)]
                    parts.append(jnp.where(slot > 0, tile, 0.0))
                dense[a, block(i), pl.ds(0, cols)] = jnp.concatenate(parts, axis=1)
                return carry

            lax.fori_loop(0, half, one, 0)
            put(down, place if a == 0 else 1 - place, pl.ds(a * rows, rows), dense[a, pl.ds(0, rows), :])

    def put(panels, turned, there, panel):
        depth = panel.shape[1]
        high, low = halves(panel)
        panels[there, pl.ds(pl.multiple_of(turned * depth, 128), depth)] = high
        panels[there, pl.ds(pl.multiple_of((turned + 2) * depth, 128), depth)] = low

    def turn(place):
        there = pl.ds(pl.multiple_of(place * cols, 16), cols)
        for a in range(2):
            put(upward, place if a == 0 else 1 - place, there, dense[a].T[:cols])

    fill(0, h)
    turn(h)
    awaited(4, 1).wait_recv()
    other_slots = pltpu.make_async_copy(slots.at[1], slots_smem.at[1], load_sem.at[5])
    other_slots.start()
    other_slots.wait()
    awaited(4, 0).wait_recv()
    pieces = []
    for k in range(stored // 2):
        pair = packed[1, k]
        tiles[1, 2 * k] = pair[:, :orb]
        tiles[1, 2 * k + 1] = pair[:, orb : 2 * orb]
        if k * part < orb:
            pieces.append(pair[:, 2 * orb : 2 * orb + min(part, orb - k * part)])
    diags[1] = jnp.concatenate(pieces, axis=1)
    fill(1, other)

    diag_left = halves(jnp.where(h == 0, diags[0], diags[1]))
    diag_right = halves(jnp.where(h == 0, diags[1], diags[0]))

    centre = 0.5 * (filter_high + filter_low)
    half_width = 0.5 * (filter_high - filter_low)

    def one_step(step, carry):
        previous, own = carry
        awaited(0, step).wait_recv()
        direct[step] = mix(down, col_field[step], left)
        for d, slot in enumerate(col_slots):
            copy(1, step, direct.at[step, block(slot)], direct_in.at[step, d], (r, h * half + slot)).start()

        @pl.when(step == 0)
        def _():
            turn(other)

        @pl.when(step > 0)
        def _():
            awaited(3, step).wait_recv()

        mirror[step] = mix(upward, row_field[step], left)
        for d, peer in enumerate(row_peers):
            copy(2, step, mirror.at[step, block(peer)], mirror_in.at[step, d], (peer, c)).start()
        image = jnp.where(left, product(*diag_left, own), product(*diag_right, own))
        image = image + direct[step, block(m), :] + mirror[step, block(r), :]
        awaited(1, step).wait_recv()
        for d in range(half - 1):
            image = image + direct_in[step, d]
        awaited(2, step).wait_recv()
        for d in range(n_row - 1):
            image = image + mirror_in[step, d]
        shifted = (image - centre * own) / half_width
        following = jnp.where(step == 0, shifted, 2.0 * shifted - previous)

        @pl.when(step < DEGREE - 1)
        def _():
            row_field[step + 1, block(m), :] = following
            col_field[step + 1, block(r), :] = following
            mine = row_field.at[step + 1, block(m)]
            for peer in row_peers:
                copy(0, step + 1, mine, col_field.at[step + 1, block(r)], (peer, c)).start()
            for slot in col_slots:
                copy(3, step + 1, mine, mine, (r, h * half + slot)).start()

        return own, following

    _, own = lax.fori_loop(0, DEGREE, one_step, (jnp.zeros_like(own), own))
    final[h, block(m), :] = own
    mine, theirs = final.at[h, block(m)], final.at[other, block(m)]
    copy(4, 2, mine, mine, (r, partner)).start()
    for slot in col_slots:
        copy(3, 0, mine, mine, (r, h * half + slot)).start()
    awaited(4, 2).wait_recv()
    for slot in col_slots:
        copy(4, 3, theirs, theirs, (r, h * half + slot)).start()
    awaited(3, 0).wait_recv()
    awaited(4, 3).wait_recv()
    low, high = final[0], final[1]
    out_ref[pl.ds(0, rows), :] = jnp.where(left, low, pltpu.roll(high, width // 2, 1))
    out_ref[pl.ds(rows, rows), :] = jnp.where(left, pltpu.roll(low, width // 2, 1), high)
    for kind in range(5):
        for step in range(4 if kind == 4 else DEGREE):
            awaited(kind, step).wait_send()


def up(value, unit):
    return (value + unit - 1) // unit * unit


def body(n_row, n_col, vectors, tiles, tile_pos, diag_blocks):
    tile_data = tiles[0, 0]
    stored, orb, _ = tile_data.shape
    width = vectors.shape[1]
    half = n_col // 2
    rows, cols = half * orb, n_row * orb
    hbm = pl.BlockSpec(memory_space=pl.ANY)
    f32, bf16, i32 = jnp.float32, jnp.bfloat16, jnp.int32
    tall, broad = up(rows, 128), up(cols, 128)
    return pl.pallas_call(
        functools.partial(kernel, n_row, n_col),
        out_shape=jax.ShapeDtypeStruct((2 * rows, width), f32),
        in_specs=[hbm, hbm, hbm, hbm],
        out_specs=pl.BlockSpec(memory_space=pltpu.VMEM),
        scratch_shapes=[
            pltpu.SMEM(tile_pos.shape[2:], i32),
            pltpu.VMEM((2, n_col, 128), i32),
            pltpu.SMEM((2, n_col, 128), i32),
            pltpu.VMEM((2 * rows, width), f32),
            pltpu.VMEM((2, stored, orb, orb), f32),
            pltpu.VMEM((2, orb, orb), f32),
            pltpu.VMEM((2, stored // 2, orb, width), f32),
            pltpu.VMEM((2, tall, broad), f32),
            pltpu.VMEM((2 * rows, 4 * broad), bf16),
            pltpu.VMEM((2 * cols, 4 * tall), bf16),
            pltpu.VMEM((DEGREE, cols, width), f32),
            pltpu.VMEM((DEGREE, rows, width), f32),
            pltpu.VMEM((2, rows, width), f32),
            pltpu.VMEM((DEGREE, rows, width), f32),
            pltpu.VMEM((DEGREE, cols, width), f32),
            pltpu.VMEM((DEGREE, half - 1, orb, width), f32),
            pltpu.VMEM((DEGREE, n_row - 1, orb, width), f32),
            pltpu.SemaphoreType.DMA((6,)),
            pltpu.SemaphoreType.DMA((5, 4)),
            pltpu.SemaphoreType.DMA((5, 4)),
        ],
        compiler_params=pltpu.CompilerParams(
            collective_id=0, has_side_effects=True, vmem_limit_bytes=56 * 1024 * 1024
        ),
        cost_estimate=pl.CostEstimate(
            flops=16 * DEGREE * rows * cols * width, bytes_accessed=8 * rows * width, transcendentals=0
        ),
    )(tile_pos[0, 0], vectors, tile_data, diag_blocks[0])


def solution(mesh):
    return jax.shard_map(
        functools.partial(body, mesh.shape["row"], mesh.shape["col"]),
        mesh=mesh,
        in_specs=(
            P("row", None),
            P("row", "col", None, None, None),
            P("row", "col", None, None),
            P(("row", "col"), None, None),
        ),
        out_specs=P("row", None),
        check_vma=False,
    )
```

```python
import functools

import jax
import jax.numpy as jnp
from jax import lax
from jax.experimental import pallas as pl
from jax.experimental.pallas import tpu as pltpu
from jax.sharding import PartitionSpec as P

DEGREE = 3
MESH = pl.DeviceIdType.MESH

filter_low = 0.0
filter_high = 8.0


def halves(value):
    high = value.astype(jnp.bfloat16)
    return high, (value - high.astype(jnp.float32)).astype(jnp.bfloat16)


def product(left_high, left_low, right):
    right_high, right_low = halves(right)
    dot = functools.partial(jnp.dot, preferred_element_type=jnp.float32)
    return dot(left_high, right_high) + (dot(left_high, right_low) + dot(left_low, right_high))


def mix(high, low, field, left):
    far = pltpu.roll(field, field.shape[1] // 2, 1)
    both = product(high[0], low[0], field) + product(high[1], low[1], far)
    count = both.shape[0] // 2
    return jnp.where(left, both[:count], both[count:])


def kernel(
    n_row, n_col, pos_hbm, vectors_hbm, tiles_hbm, diag_hbm, out_ref,
    pos, slots, slots_smem, vectors, tiles, diags, packed, dense,
    down_h, down_l, up_h, up_l,
    col_field, row_field, final, direct, mirror, direct_in, mirror_in,
    load_sem, send_sem, recv_sem,
):
    orb = diag_hbm.shape[0]
    width = vectors.shape[1]
    stored = tiles.shape[1]
    half = n_col // 2
    rows, cols = half * orb, n_row * orb
    r, c = lax.axis_index("row"), lax.axis_index("col")
    h, m = c // half, c % half
    other = 1 - h
    partner = other * half + m
    row_peers = [lax.rem(r + d, n_row) for d in range(1, n_row)]
    col_slots = [lax.rem(m + d, half) for d in range(1, half)]
    left = lax.broadcasted_iota(jnp.int32, (1, width), 1) < width // 2

    def block(index):
        return pl.ds(pl.multiple_of(index * orb, 8), orb)

    loads = [
        pltpu.make_async_copy(pos_hbm, pos, load_sem.at[0]),
        pltpu.make_async_copy(vectors_hbm, vectors, load_sem.at[1]),
        pltpu.make_async_copy(tiles_hbm, tiles.at[0], load_sem.at[2]),
        pltpu.make_async_copy(diag_hbm, diags.at[0], load_sem.at[3]),
    ]
    for load in loads:
        load.start()

    barrier = pltpu.get_barrier_semaphore()
    for peer in row_peers:
        pl.semaphore_signal(barrier, inc=1, device_id=(peer, c), device_id_type=MESH)
    for slot in col_slots:
        pl.semaphore_signal(barrier, inc=1, device_id=(r, h * half + slot), device_id_type=MESH)
    for slot in [m] + col_slots:
        pl.semaphore_signal(barrier, inc=1, device_id=(r, other * half + slot), device_id_type=MESH)

    def copy(kind, step, source, target, device):
        return pltpu.make_async_remote_copy(
            src_ref=source, dst_ref=target,
            send_sem=send_sem.at[kind, step], recv_sem=recv_sem.at[kind, step],
            device_id=device, device_id_type=MESH,
        )

    def region_of(kind, step):
        if kind == 0:
            return col_field.at[step, pl.ds(0, cols - orb)]
        if kind == 1:
            return direct_in.at[step]
        if kind == 2:
            return mirror_in.at[step]
        if kind == 3:
            return row_field.at[step, pl.ds(0, rows - orb)]
        if step == 0:
            return packed.at[1]
        if step == 1:
            return slots.at[1]
        return final.at[0]

    def awaited(kind, step):
        region = region_of(kind, step)
        return copy(kind, step, region, region, (r, c))

    loads[2].wait()
    loads[3].wait()
    part = (width - 2 * orb) // 8 * 8
    for k in range(stored // 2):
        pieces = [tiles[0, 2 * k], tiles[0, 2 * k + 1]]
        if k * part < orb:
            share = min(part, orb - k * part)
            pieces.append(diags[0, :, pl.ds(k * part, share)])
            if share < part:
                pieces.append(jnp.zeros((orb, part - share), jnp.float32))
        else:
            pieces.append(jnp.zeros((orb, part), jnp.float32))
        packed[0, k] = jnp.concatenate(pieces, axis=1)
    loads[0].wait()
    at_row = lax.broadcasted_iota(jnp.int32, (n_col, 128), 0)
    at_col = lax.broadcasted_iota(jnp.int32, (n_col, 128), 1)
    table = jnp.zeros((n_col, 128), jnp.int32)
    for t in range(stored):
        table = jnp.where((at_row == pos[0, t]) & (at_col == pos[1, t]), t + 1, table)
    slots[0] = table
    own_slots = pltpu.make_async_copy(slots.at[0], slots_smem.at[0], load_sem.at[4])
    own_slots.start()
    loads[1].wait()
    top, bottom = vectors[pl.ds(0, rows), :], vectors[pl.ds(rows, rows), :]
    first = jnp.where(h == 0, top, pltpu.roll(top, width // 2, 1))
    second = jnp.where(h == 0, pltpu.roll(bottom, width // 2, 1), bottom)
    row_field[0] = jnp.where(left, first, second)
    own = row_field[0, block(m), :]
    col_field[0, block(r), :] = own

    pl.semaphore_wait(barrier, n_row + n_col - 2)

    copy(4, 1, slots.at[0], slots.at[1], (r, partner)).start()
    copy(4, 0, packed.at[0], packed.at[1], (r, partner)).start()
    for peer in row_peers:
        copy(0, 0, row_field.at[0, block(m)], col_field.at[0, block(r)], (peer, c)).start()

    dense[...] = jnp.zeros_like(dense)
    own_slots.wait()

    def fill(source, place):
        for a in range(2):
            def one(i, carry):
                parts = []
                for j in range(n_row):
                    slot = slots_smem[source, a * half + i, j]
                    tile = tiles[source, jnp.maximum(slot - 1, 0)]
                    parts.append(jnp.where(slot > 0, tile, 0.0))
                dense[a, block(i), pl.ds(0, cols)] = jnp.concatenate(parts, axis=1)
                return carry

            lax.fori_loop(0, half, one, 0)
            turned = place if a == 0 else 1 - place
            panel = dense[a]
            there = pl.ds(a * rows, rows)
            down_h[turned, there, :], down_l[turned, there, :] = halves(panel[:rows, :cols])
            there = pl.ds(pl.multiple_of(place * cols, 16), cols)
            up_h[turned, there, :], up_l[turned, there, :] = halves(panel.T[:cols, :rows])

    fill(0, h)
    awaited(4, 1).wait_recv()
    other_slots = pltpu.make_async_copy(slots.at[1], slots_smem.at[1], load_sem.at[5])
    other_slots.start()
    other_slots.wait()
    awaited(4, 0).wait_recv()
    pieces = []
    for k in range(stored // 2):
        pair = packed[1, k]
        tiles[1, 2 * k] = pair[:, :orb]
        tiles[1, 2 * k + 1] = pair[:, orb : 2 * orb]
        if k * part < orb:
            pieces.append(pair[:, 2 * orb : 2 * orb + min(part, orb - k * part)])
    diags[1] = jnp.concatenate(pieces, axis=1)
    fill(1, other)

    diag_left = halves(jnp.where(h == 0, diags[0], diags[1]))
    diag_right = halves(jnp.where(h == 0, diags[1], diags[0]))

    centre = 0.5 * (filter_high + filter_low)
    half_width = 0.5 * (filter_high - filter_low)

    def one_step(step, carry):
        previous, own = carry
        awaited(0, step).wait_recv()
        direct[step] = mix(down_h, down_l, col_field[step], left)
        for d, slot in enumerate(col_slots):
            copy(1, step, direct.at[step, block(slot)], direct_in.at[step, d], (r, h * half + slot)).start()

        @pl.when(step > 0)
        def _():
            awaited(3, step).wait_recv()

        mirror[step] = mix(up_h, up_l, row_field[step], left)
        for d, peer in enumerate(row_peers):
            copy(2, step, mirror.at[step, block(peer)], mirror_in.at[step, d], (peer, c)).start()
        image = jnp.where(left, product(*diag_left, own), product(*diag_right, own))
        image = image + direct[step, block(m), :] + mirror[step, block(r), :]
        awaited(1, step).wait_recv()
        for d in range(half - 1):
            image = image + direct_in[step, d]
        awaited(2, step).wait_recv()
        for d in range(n_row - 1):
            image = image + mirror_in[step, d]
        shifted = (image - centre * own) / half_width
        following = jnp.where(step == 0, shifted, 2.0 * shifted - previous)

        @pl.when(step < DEGREE - 1)
        def _():
            row_field[step + 1, block(m), :] = following
            col_field[step + 1, block(r), :] = following
            mine = row_field.at[step + 1, block(m)]
            for peer in row_peers:
                copy(0, step + 1, mine, col_field.at[step + 1, block(r)], (peer, c)).start()
            for slot in col_slots:
                copy(3, step + 1, mine, mine, (r, h * half + slot)).start()

        return own, following

    _, own = lax.fori_loop(0, DEGREE, one_step, (jnp.zeros_like(own), own))
    final[h, block(m), :] = 0.5 * own
    mine = final.at[h, block(m)]
    for slot in [m] + col_slots:
        copy(4, 2, mine, mine, (r, other * half + slot)).start()
    for slot in col_slots:
        copy(3, 0, mine, mine, (r, h * half + slot)).start()
    awaited(3, 0).wait_recv()
    awaited(4, 2).wait_recv()
    low, high = final[0], final[1]
    out_ref[pl.ds(0, rows), :] = jnp.where(left, low, pltpu.roll(high, width // 2, 1))
    out_ref[pl.ds(rows, rows), :] = jnp.where(left, pltpu.roll(low, width // 2, 1), high)
    for kind in range(5):
        for step in range(DEGREE):
            awaited(kind, step).wait_send()


def up(value, unit):
    return (value + unit - 1) // unit * unit


def body(n_row, n_col, vectors, tiles, tile_pos, diag_blocks):
    tile_data = tiles[0, 0]
    stored, orb, _ = tile_data.shape
    width = vectors.shape[1]
    half = n_col // 2
    rows, cols = half * orb, n_row * orb
    hbm = pl.BlockSpec(memory_space=pl.ANY)
    f32, bf16, i32 = jnp.float32, jnp.bfloat16, jnp.int32
    down = pltpu.VMEM((2, 2 * rows, cols), bf16)
    upward = pltpu.VMEM((2, 2 * cols, rows), bf16)
    halved = pl.pallas_call(
        functools.partial(kernel, n_row, n_col),
        out_shape=jax.ShapeDtypeStruct((2 * rows, width), f32),
        in_specs=[hbm, hbm, hbm, hbm],
        out_specs=pl.BlockSpec(memory_space=pltpu.VMEM),
        scratch_shapes=[
            pltpu.SMEM(tile_pos.shape[2:], i32),
            pltpu.VMEM((2, n_col, 128), i32),
            pltpu.SMEM((2, n_col, 128), i32),
            pltpu.VMEM((2 * rows, width), f32),
            pltpu.VMEM((2, stored, orb, orb), f32),
            pltpu.VMEM((2, orb, orb), f32),
            pltpu.VMEM((2, stored // 2, orb, width), f32),
            pltpu.VMEM((2, up(rows, 128), up(cols, 128)), f32),
            down, down, upward, upward,
            pltpu.VMEM((DEGREE, cols, width), f32),
            pltpu.VMEM((DEGREE, rows, width), f32),
            pltpu.VMEM((2, rows, width), f32),
            pltpu.VMEM((DEGREE, rows, width), f32),
            pltpu.VMEM((DEGREE, cols, width), f32),
            pltpu.VMEM((DEGREE, half - 1, orb, width), f32),
            pltpu.VMEM((DEGREE, n_row - 1, orb, width), f32),
            pltpu.SemaphoreType.DMA((6,)),
            pltpu.SemaphoreType.DMA((5, 4)),
            pltpu.SemaphoreType.DMA((5, 4)),
        ],
        compiler_params=pltpu.CompilerParams(
            collective_id=0, has_side_effects=True, vmem_limit_bytes=56 * 1024 * 1024
        ),
        cost_estimate=pl.CostEstimate(
            flops=16 * DEGREE * rows * cols * width, bytes_accessed=8 * rows * width, transcendentals=0
        ),
    )(tile_pos[0, 0], vectors, tile_data, diag_blocks[0])
    return 2.0 * halved


def solution(mesh):
    return jax.shard_map(
        functools.partial(body, mesh.shape["row"], mesh.shape["col"]),
        mesh=mesh,
        in_specs=(
            P("row", None),
            P("row", "col", None, None, None),
            P("row", "col", None, None),
            P(("row", "col"), None, None),
        ),
        out_specs=P("row", None),
        check_vma=False,
    )
```

```python
import functools

import jax
import jax.numpy as jnp
from jax import lax
from jax.experimental import pallas as pl
from jax.experimental.pallas import tpu as pltpu
from jax.sharding import PartitionSpec as P

DEGREE = 3
MESH = pl.DeviceIdType.MESH

filter_low = 0.0
filter_high = 8.0


def halves(value):
    high = value.astype(jnp.bfloat16)
    return high, (value - high.astype(jnp.float32)).astype(jnp.bfloat16)


def product(left_high, left_low, right):
    right_high, right_low = halves(right)
    dot = functools.partial(jnp.dot, preferred_element_type=jnp.float32)
    return dot(left_high, right_high) + (dot(left_high, right_low) + dot(left_low, right_high))


def mix(panels, field, left):
    count, width = field.shape
    depth = panels.shape[1] // 4
    turn = functools.partial(pltpu.roll, shift=width // 2, axis=1)
    high = field.astype(jnp.bfloat16).astype(jnp.float32)
    low = field - high
    pieces = [jnp.where(left, high, turn(low)), jnp.where(left, turn(high), low)]
    if depth > count:
        empty = jnp.zeros((depth - count, width), jnp.float32)
        pieces = [pieces[0], empty, pieces[1], empty]
    right = jnp.concatenate(pieces, axis=0).astype(jnp.bfloat16)
    both = jnp.dot(panels[...], jnp.concatenate([right, right], axis=0), preferred_element_type=jnp.float32)
    both = both + turn(both)
    count = both.shape[0] // 2
    return jnp.where(left, both[:count], both[count:])


def kernel(
    n_row, n_col, pos_hbm, vectors_hbm, tiles_hbm, diag_hbm, out_ref,
    pos, slots, slots_smem, vectors, tiles, diags, packed, dense,
    down, upward,
    col_field, row_field, final, direct, mirror, direct_in, mirror_in,
    load_sem, send_sem, recv_sem,
):
    orb = diag_hbm.shape[0]
    width = vectors.shape[1]
    stored = tiles.shape[1]
    half = n_col // 2
    rows, cols = half * orb, n_row * orb
    r, c = lax.axis_index("row"), lax.axis_index("col")
    h, m = c // half, c % half
    other = 1 - h
    partner = other * half + m
    row_peers = [lax.rem(r + d, n_row) for d in range(1, n_row)]
    col_slots = [lax.rem(m + d, half) for d in range(1, half)]
    left = lax.broadcasted_iota(jnp.int32, (1, width), 1) < width // 2

    def block(index):
        return pl.ds(pl.multiple_of(index * orb, 8), orb)

    loads = [
        pltpu.make_async_copy(pos_hbm, pos, load_sem.at[0]),
        pltpu.make_async_copy(vectors_hbm, vectors, load_sem.at[1]),
        pltpu.make_async_copy(tiles_hbm, tiles.at[0], load_sem.at[2]),
        pltpu.make_async_copy(diag_hbm, diags.at[0], load_sem.at[3]),
    ]
    for load in loads:
        load.start()

    barrier = pltpu.get_barrier_semaphore()
    for peer in row_peers:
        pl.semaphore_signal(barrier, inc=1, device_id=(peer, c), device_id_type=MESH)
    for slot in col_slots:
        pl.semaphore_signal(barrier, inc=1, device_id=(r, h * half + slot), device_id_type=MESH)
    pl.semaphore_signal(barrier, inc=1, device_id=(r, partner), device_id_type=MESH)

    def copy(kind, step, source, target, device):
        return pltpu.make_async_remote_copy(
            src_ref=source, dst_ref=target,
            send_sem=send_sem.at[kind, step], recv_sem=recv_sem.at[kind, step],
            device_id=device, device_id_type=MESH,
        )

    def region_of(kind, step):
        if kind == 0:
            return col_field.at[step, pl.ds(0, cols - orb)]
        if kind == 1:
            return direct_in.at[step]
        if kind == 2:
            return mirror_in.at[step]
        if kind == 3:
            return row_field.at[step, pl.ds(0, rows - orb)]
        if step == 3:
            return final.at[0, pl.ds(0, rows - orb)]
        if step == 0:
            return packed.at[1]
        if step == 1:
            return slots.at[1]
        return final.at[0, pl.ds(0, orb)]

    def awaited(kind, step):
        region = region_of(kind, step)
        return copy(kind, step, region, region, (r, c))

    loads[2].wait()
    loads[3].wait()
    part = (width - 2 * orb) // 8 * 8
    for k in range(stored // 2):
        pieces = [tiles[0, 2 * k], tiles[0, 2 * k + 1]]
        if k * part < orb:
            share = min(part, orb - k * part)
            pieces.append(diags[0, :, pl.ds(k * part, share)])
            if share < part:
                pieces.append(jnp.zeros((orb, part - share), jnp.float32))
        else:
            pieces.append(jnp.zeros((orb, part), jnp.float32))
        packed[0, k] = jnp.concatenate(pieces, axis=1)
    loads[0].wait()
    at_row = lax.broadcasted_iota(jnp.int32, (n_col, 128), 0)
    at_col = lax.broadcasted_iota(jnp.int32, (n_col, 128), 1)
    table = jnp.zeros((n_col, 128), jnp.int32)
    for t in range(stored):
        table = jnp.where((at_row == pos[0, t]) & (at_col == pos[1, t]), t + 1, table)
    slots[0] = table
    own_slots = pltpu.make_async_copy(slots.at[0], slots_smem.at[0], load_sem.at[4])
    own_slots.start()
    loads[1].wait()
    top, bottom = vectors[pl.ds(0, rows), :], vectors[pl.ds(rows, rows), :]
    first = jnp.where(h == 0, top, pltpu.roll(top, width // 2, 1))
    second = jnp.where(h == 0, pltpu.roll(bottom, width // 2, 1), bottom)
    row_field[0] = jnp.where(left, first, second)
    own = row_field[0, block(m), :]
    col_field[0, block(r), :] = own

    pl.semaphore_wait(barrier, n_row + half - 1)

    copy(4, 1, slots.at[0], slots.at[1], (r, partner)).start()
    copy(4, 0, packed.at[0], packed.at[1], (r, partner)).start()
    for peer in row_peers:
        copy(0, 0, row_field.at[0, block(m)], col_field.at[0, block(r)], (peer, c)).start()

    dense[...] = jnp.zeros_like(dense)
    own_slots.wait()

    def fill(source, place):
        for a in range(2):
            def one(i, carry):
                parts = []
                for j in range(n_row):
                    slot = slots_smem[source, a * half + i, j]
                    tile = tiles[source, jnp.maximum(slot - 1, 0)]
                    parts.append(jnp.where(slot > 0, tile, 0.0))
                dense[a, block(i), pl.ds(0, cols)] = jnp.concatenate(parts, axis=1)
                return carry

            lax.fori_loop(0, half, one, 0)
            put(down, place, pl.ds(a * rows, rows), dense[a, pl.ds(0, rows), :])

    def put(panels, part, there, panel):
        depth = panel.shape[1]
        high, low = halves(panel)
        panels[there, pl.ds(pl.multiple_of(part * depth, 128), depth)] = high
        panels[there, pl.ds(pl.multiple_of((part + 2) * depth, 128), depth)] = low

    def turn(place):
        there = pl.ds(pl.multiple_of(place * cols, 16), cols)
        for a in range(2):
            put(upward, a, there, dense[a].T[:cols])

    fill(0, h)
    turn(h)
    awaited(4, 1).wait_recv()
    other_slots = pltpu.make_async_copy(slots.at[1], slots_smem.at[1], load_sem.at[5])
    other_slots.start()
    other_slots.wait()
    awaited(4, 0).wait_recv()
    pieces = []
    for k in range(stored // 2):
        pair = packed[1, k]
        tiles[1, 2 * k] = pair[:, :orb]
        tiles[1, 2 * k + 1] = pair[:, orb : 2 * orb]
        if k * part < orb:
            pieces.append(pair[:, 2 * orb : 2 * orb + min(part, orb - k * part)])
    diags[1] = jnp.concatenate(pieces, axis=1)
    fill(1, other)

    diag_left = halves(jnp.where(h == 0, diags[0], diags[1]))
    diag_right = halves(jnp.where(h == 0, diags[1], diags[0]))

    centre = 0.5 * (filter_high + filter_low)
    half_width = 0.5 * (filter_high - filter_low)

    def one_step(step, carry):
        previous, own = carry
        awaited(0, step).wait_recv()
        direct[step] = mix(down, col_field[step], left)
        for d, slot in enumerate(col_slots):
            copy(1, step, direct.at[step, block(slot)], direct_in.at[step, d], (r, h * half + slot)).start()

        @pl.when(step == 0)
        def _():
            turn(other)

        @pl.when(step > 0)
        def _():
            awaited(3, step).wait_recv()

        mirror[step] = mix(upward, row_field[step], left)
        for d, peer in enumerate(row_peers):
            copy(2, step, mirror.at[step, block(peer)], mirror_in.at[step, d], (peer, c)).start()
        image = jnp.where(left, product(*diag_left, own), product(*diag_right, own))
        image = image + direct[step, block(m), :] + mirror[step, block(r), :]
        awaited(1, step).wait_recv()
        for d in range(half - 1):
            image = image + direct_in[step, d]
        awaited(2, step).wait_recv()
        for d in range(n_row - 1):
            image = image + mirror_in[step, d]
        shifted = (image - centre * own) / half_width
        following = jnp.where(step == 0, shifted, 2.0 * shifted - previous)

        @pl.when(step < DEGREE - 1)
        def _():
            row_field[step + 1, block(m), :] = following
            col_field[step + 1, block(r), :] = following
            mine = row_field.at[step + 1, block(m)]
            for peer in row_peers:
                copy(0, step + 1, mine, col_field.at[step + 1, block(r)], (peer, c)).start()
            for slot in col_slots:
                copy(3, step + 1, mine, mine, (r, h * half + slot)).start()

        return own, following

    _, own = lax.fori_loop(0, DEGREE, one_step, (jnp.zeros_like(own), own))
    final[h, block(m), :] = own
    mine, theirs = final.at[h, block(m)], final.at[other, block(m)]
    copy(4, 2, mine, mine, (r, partner)).start()
    for slot in col_slots:
        copy(3, 0, mine, mine, (r, h * half + slot)).start()
    awaited(4, 2).wait_recv()
    for slot in col_slots:
        copy(4, 3, theirs, theirs, (r, h * half + slot)).start()
    awaited(3, 0).wait_recv()
    awaited(4, 3).wait_recv()
    low, high = final[0], final[1]
    out_ref[pl.ds(0, rows), :] = jnp.where(left, low, pltpu.roll(high, width // 2, 1))
    out_ref[pl.ds(rows, rows), :] = jnp.where(left, pltpu.roll(low, width // 2, 1), high)
    for kind in range(5):
        for step in range(4 if kind == 4 else DEGREE):
            awaited(kind, step).wait_send()


def up(value, unit):
    return (value + unit - 1) // unit * unit


def body(n_row, n_col, vectors, tiles, tile_pos, diag_blocks):
    tile_data = tiles[0, 0]
    stored, orb, _ = tile_data.shape
    width = vectors.shape[1]
    half = n_col // 2
    rows, cols = half * orb, n_row * orb
    hbm = pl.BlockSpec(memory_space=pl.ANY)
    f32, bf16, i32 = jnp.float32, jnp.bfloat16, jnp.int32
    tall, broad = up(rows, 128), up(cols, 128)
    return pl.pallas_call(
        functools.partial(kernel, n_row, n_col),
        out_shape=jax.ShapeDtypeStruct((2 * rows, width), f32),
        in_specs=[hbm, hbm, hbm, hbm],
        out_specs=pl.BlockSpec(memory_space=pltpu.VMEM),
        scratch_shapes=[
            pltpu.SMEM(tile_pos.shape[2:], i32),
            pltpu.VMEM((2, n_col, 128), i32),
            pltpu.SMEM((2, n_col, 128), i32),
            pltpu.VMEM((2 * rows, width), f32),
            pltpu.VMEM((2, stored, orb, orb), f32),
            pltpu.VMEM((2, orb, orb), f32),
            pltpu.VMEM((2, stored // 2, orb, width), f32),
            pltpu.VMEM((2, tall, broad), f32),
            pltpu.VMEM((2 * rows, 4 * broad), bf16),
            pltpu.VMEM((2 * cols, 4 * tall), bf16),
            pltpu.VMEM((DEGREE, cols, width), f32),
            pltpu.VMEM((DEGREE, rows, width), f32),
            pltpu.VMEM((2, rows, width), f32),
            pltpu.VMEM((DEGREE, rows, width), f32),
            pltpu.VMEM((DEGREE, cols, width), f32),
            pltpu.VMEM((DEGREE, half - 1, orb, width), f32),
            pltpu.VMEM((DEGREE, n_row - 1, orb, width), f32),
            pltpu.SemaphoreType.DMA((6,)),
            pltpu.SemaphoreType.DMA((5, 4)),
            pltpu.SemaphoreType.DMA((5, 4)),
        ],
        compiler_params=pltpu.CompilerParams(
            collective_id=0, has_side_effects=True, vmem_limit_bytes=56 * 1024 * 1024
        ),
        cost_estimate=pl.CostEstimate(
            flops=16 * DEGREE * rows * cols * width, bytes_accessed=8 * rows * width, transcendentals=0
        ),
    )(tile_pos[0, 0], vectors, tile_data, diag_blocks[0])


def solution(mesh):
    return jax.shard_map(
        functools.partial(body, mesh.shape["row"], mesh.shape["col"]),
        mesh=mesh,
        in_specs=(
            P("row", None),
            P("row", "col", None, None, None),
            P("row", "col", None, None),
            P(("row", "col"), None, None),
        ),
        out_specs=P("row", None),
        check_vma=False,
    )
```

```python
import functools

import jax
import jax.numpy as jnp
from jax import lax
from jax.experimental import pallas as pl
from jax.experimental.pallas import tpu as pltpu
from jax.sharding import PartitionSpec as P

DEGREE = 3
MESH = pl.DeviceIdType.MESH

filter_low = 0.0
filter_high = 8.0


def halves(value):
    high = value.astype(jnp.bfloat16)
    return high, (value - high.astype(jnp.float32)).astype(jnp.bfloat16)


def product(left_high, left_low, right):
    right_high, right_low = halves(right)
    dot = functools.partial(jnp.dot, preferred_element_type=jnp.float32)
    return dot(left_high, right_high) + (dot(left_high, right_low) + dot(left_low, right_high))


def mix(panels, field, left):
    count, width = field.shape
    depth = panels.shape[1] // 4
    turn = functools.partial(pltpu.roll, shift=width // 2, axis=1)
    high = field.astype(jnp.bfloat16).astype(jnp.float32)
    low = field - high
    pieces = [jnp.where(left, high, turn(low)), jnp.where(left, turn(high), low)]
    if depth > count:
        empty = jnp.zeros((depth - count, width), jnp.float32)
        pieces = [pieces[0], empty, pieces[1], empty]
    right = jnp.concatenate(pieces, axis=0).astype(jnp.bfloat16)
    both = jnp.dot(panels[...], jnp.concatenate([right, right], axis=0), preferred_element_type=jnp.float32)
    both = both + turn(both)
    count = both.shape[0] // 2
    return jnp.where(left, both[:count], both[count:])


def kernel(
    n_row, n_col, pos_hbm, vectors_hbm, tiles_hbm, diag_hbm, out_ref,
    pos, slots, slots_smem, vectors, tiles, diags, packed, dense,
    down, upward,
    col_field, row_field, final, direct, mirror, direct_in, mirror_in,
    load_sem, send_sem, recv_sem,
):
    orb = diag_hbm.shape[0]
    width = vectors.shape[1]
    stored = tiles.shape[1]
    half = n_col // 2
    rows, cols = half * orb, n_row * orb
    r, c = lax.axis_index("row"), lax.axis_index("col")
    h, m = c // half, c % half
    other = 1 - h
    partner = other * half + m
    row_peers = [lax.rem(r + d, n_row) for d in range(1, n_row)]
    col_slots = [lax.rem(m + d, half) for d in range(1, half)]
    left = lax.broadcasted_iota(jnp.int32, (1, width), 1) < width // 2

    def block(index):
        return pl.ds(pl.multiple_of(index * orb, 8), orb)

    loads = [
        pltpu.make_async_copy(pos_hbm, pos, load_sem.at[0]),
        pltpu.make_async_copy(vectors_hbm, vectors, load_sem.at[1]),
        pltpu.make_async_copy(tiles_hbm, tiles.at[0], load_sem.at[2]),
        pltpu.make_async_copy(diag_hbm, diags.at[0], load_sem.at[3]),
    ]
    for load in loads:
        load.start()

    barrier = pltpu.get_barrier_semaphore()
    for peer in row_peers:
        pl.semaphore_signal(barrier, inc=1, device_id=(peer, c), device_id_type=MESH)
    for slot in col_slots:
        pl.semaphore_signal(barrier, inc=1, device_id=(r, h * half + slot), device_id_type=MESH)
    pl.semaphore_signal(barrier, inc=1, device_id=(r, partner), device_id_type=MESH)

    def copy(kind, step, source, target, device):
        return pltpu.make_async_remote_copy(
            src_ref=source, dst_ref=target,
            send_sem=send_sem.at[kind, step], recv_sem=recv_sem.at[kind, step],
            device_id=device, device_id_type=MESH,
        )

    cut = orb // 16 * 8
    shares = ((0, cut), (cut, orb - cut))

    def region_of(kind, step):
        if kind == 0:
            return col_field.at[step, pl.ds(0, cols - orb)]
        if kind == 1:
            return direct_in.at[step]
        if kind == 2:
            return mirror_in.at[step]
        if kind == 3:
            return row_field.at[step, pl.ds(0, rows - orb)]
        if step == 0:
            return packed.at[1]
        if step == 1:
            return slots.at[1]
        size = shares[step // 2 - 1][1]
        return final.at[0, pl.ds(0, size * (half - 1 if step % 2 == 1 else 1))]

    def awaited(kind, step):
        region = region_of(kind, step)
        return copy(kind, step, region, region, (r, c))

    loads[2].wait()
    loads[3].wait()
    part = (width - 2 * orb) // 8 * 8
    for k in range(stored // 2):
        pieces = [tiles[0, 2 * k], tiles[0, 2 * k + 1]]
        if k * part < orb:
            share = min(part, orb - k * part)
            pieces.append(diags[0, :, pl.ds(k * part, share)])
            if share < part:
                pieces.append(jnp.zeros((orb, part - share), jnp.float32))
        else:
            pieces.append(jnp.zeros((orb, part), jnp.float32))
        packed[0, k] = jnp.concatenate(pieces, axis=1)
    loads[0].wait()
    at_row = lax.broadcasted_iota(jnp.int32, (n_col, 128), 0)
    at_col = lax.broadcasted_iota(jnp.int32, (n_col, 128), 1)
    table = jnp.zeros((n_col, 128), jnp.int32)
    for t in range(stored):
        table = jnp.where((at_row == pos[0, t]) & (at_col == pos[1, t]), t + 1, table)
    slots[0] = table
    own_slots = pltpu.make_async_copy(slots.at[0], slots_smem.at[0], load_sem.at[4])
    own_slots.start()
    loads[1].wait()
    top, bottom = vectors[pl.ds(0, rows), :], vectors[pl.ds(rows, rows), :]
    first = jnp.where(h == 0, top, pltpu.roll(top, width // 2, 1))
    second = jnp.where(h == 0, pltpu.roll(bottom, width // 2, 1), bottom)
    row_field[0] = jnp.where(left, first, second)
    own = row_field[0, block(m), :]
    col_field[0, block(r), :] = own

    pl.semaphore_wait(barrier, n_row + half - 1)

    copy(4, 1, slots.at[0], slots.at[1], (r, partner)).start()
    copy(4, 0, packed.at[0], packed.at[1], (r, partner)).start()
    for peer in row_peers:
        copy(0, 0, row_field.at[0, block(m)], col_field.at[0, block(r)], (peer, c)).start()

    dense[...] = jnp.zeros_like(dense)
    own_slots.wait()

    def fill(source, place):
        for a in range(2):
            def one(i, carry):
                parts = []
                for j in range(n_row):
                    slot = slots_smem[source, a * half + i, j]
                    tile = tiles[source, jnp.maximum(slot - 1, 0)]
                    parts.append(jnp.where(slot > 0, tile, 0.0))
                dense[a, block(i), pl.ds(0, cols)] = jnp.concatenate(parts, axis=1)
                return carry

            lax.fori_loop(0, half, one, 0)
            put(down, place, pl.ds(a * rows, rows), dense[a, pl.ds(0, rows), :])

    def put(panels, part, there, panel):
        depth = panel.shape[1]
        high, low = halves(panel)
        panels[there, pl.ds(pl.multiple_of(part * depth, 128), depth)] = high
        panels[there, pl.ds(pl.multiple_of((part + 2) * depth, 128), depth)] = low

    def turn(place):
        there = pl.ds(pl.multiple_of(place * cols, 16), cols)
        for a in range(2):
            put(upward, a, there, dense[a].T[:cols])

    fill(0, h)
    turn(h)
    awaited(4, 1).wait_recv()
    other_slots = pltpu.make_async_copy(slots.at[1], slots_smem.at[1], load_sem.at[5])
    other_slots.start()
    other_slots.wait()
    awaited(4, 0).wait_recv()
    pieces = []
    for k in range(stored // 2):
        pair = packed[1, k]
        tiles[1, 2 * k] = pair[:, :orb]
        tiles[1, 2 * k + 1] = pair[:, orb : 2 * orb]
        if k * part < orb:
            pieces.append(pair[:, 2 * orb : 2 * orb + min(part, orb - k * part)])
    diags[1] = jnp.concatenate(pieces, axis=1)
    fill(1, other)

    diag_left = halves(jnp.where(h == 0, diags[0], diags[1]))
    diag_right = halves(jnp.where(h == 0, diags[1], diags[0]))

    centre = 0.5 * (filter_high + filter_low)
    half_width = 0.5 * (filter_high - filter_low)

    def one_step(step, carry):
        previous, own = carry
        awaited(0, step).wait_recv()
        direct[step] = mix(down, col_field[step], left)
        for d, slot in enumerate(col_slots):
            copy(1, step, direct.at[step, block(slot)], direct_in.at[step, d], (r, h * half + slot)).start()

        @pl.when(step == 0)
        def _():
            turn(other)

        @pl.when(step > 0)
        def _():
            awaited(3, step).wait_recv()

        mirror[step] = mix(upward, row_field[step], left)
        for d, peer in enumerate(row_peers):
            copy(2, step, mirror.at[step, block(peer)], mirror_in.at[step, d], (peer, c)).start()
        image = jnp.where(left, product(*diag_left, own), product(*diag_right, own))
        image = image + direct[step, block(m), :] + mirror[step, block(r), :]
        awaited(1, step).wait_recv()
        for d in range(half - 1):
            image = image + direct_in[step, d]
        awaited(2, step).wait_recv()
        for d in range(n_row - 1):
            image = image + mirror_in[step, d]
        shifted = (image - centre * own) / half_width
        following = jnp.where(step == 0, shifted, 2.0 * shifted - previous)

        @pl.when(step < DEGREE - 1)
        def _():
            row_field[step + 1, block(m), :] = following
            col_field[step + 1, block(r), :] = following
            mine = row_field.at[step + 1, block(m)]
            for peer in row_peers:
                copy(0, step + 1, mine, col_field.at[step + 1, block(r)], (peer, c)).start()
            for slot in col_slots:
                copy(3, step + 1, mine, mine, (r, h * half + slot)).start()

        return own, following

    _, own = lax.fori_loop(0, DEGREE, one_step, (jnp.zeros_like(own), own))
    final[h, block(m), :] = own
    mine = final.at[h, block(m)]
    for kind, (start, size) in zip((2, 4), shares):
        piece = final.at[h, pl.ds(pl.multiple_of(m * orb + start, 8), size)]
        copy(4, kind, piece, piece, (r, partner)).start()
    for slot in col_slots:
        copy(3, 0, mine, mine, (r, h * half + slot)).start()
    for kind, (start, size) in zip((2, 4), shares):
        piece = final.at[other, pl.ds(pl.multiple_of(m * orb + start, 8), size)]
        awaited(4, kind).wait_recv()
        for slot in col_slots:
            copy(4, kind + 1, piece, piece, (r, h * half + slot)).start()
    awaited(3, 0).wait_recv()
    awaited(4, 3).wait_recv()
    awaited(4, 5).wait_recv()
    low, high = final[0], final[1]
    out_ref[pl.ds(0, rows), :] = jnp.where(left, low, pltpu.roll(high, width // 2, 1))
    out_ref[pl.ds(rows, rows), :] = jnp.where(left, pltpu.roll(low, width // 2, 1), high)
    for kind in range(5):
        for step in range(6 if kind == 4 else DEGREE):
            awaited(kind, step).wait_send()


def up(value, unit):
    return (value + unit - 1) // unit * unit


def body(n_row, n_col, vectors, tiles, tile_pos, diag_blocks):
    tile_data = tiles[0, 0]
    stored, orb, _ = tile_data.shape
    width = vectors.shape[1]
    half = n_col // 2
    rows, cols = half * orb, n_row * orb
    hbm = pl.BlockSpec(memory_space=pl.ANY)
    f32, bf16, i32 = jnp.float32, jnp.bfloat16, jnp.int32
    tall, broad = up(rows, 128), up(cols, 128)
    return pl.pallas_call(
        functools.partial(kernel, n_row, n_col),
        out_shape=jax.ShapeDtypeStruct((2 * rows, width), f32),
        in_specs=[hbm, hbm, hbm, hbm],
        out_specs=pl.BlockSpec(memory_space=pltpu.VMEM),
        scratch_shapes=[
            pltpu.SMEM(tile_pos.shape[2:], i32),
            pltpu.VMEM((2, n_col, 128), i32),
            pltpu.SMEM((2, n_col, 128), i32),
            pltpu.VMEM((2 * rows, width), f32),
            pltpu.VMEM((2, stored, orb, orb), f32),
            pltpu.VMEM((2, orb, orb), f32),
            pltpu.VMEM((2, stored // 2, orb, width), f32),
            pltpu.VMEM((2, tall, broad), f32),
            pltpu.VMEM((2 * rows, 4 * broad), bf16),
            pltpu.VMEM((2 * cols, 4 * tall), bf16),
            pltpu.VMEM((DEGREE, cols, width), f32),
            pltpu.VMEM((DEGREE, rows, width), f32),
            pltpu.VMEM((2, rows, width), f32),
            pltpu.VMEM((DEGREE, rows, width), f32),
            pltpu.VMEM((DEGREE, cols, width), f32),
            pltpu.VMEM((DEGREE, half - 1, orb, width), f32),
            pltpu.VMEM((DEGREE, n_row - 1, orb, width), f32),
            pltpu.SemaphoreType.DMA((6,)),
            pltpu.SemaphoreType.DMA((5, 6)),
            pltpu.SemaphoreType.DMA((5, 6)),
        ],
        compiler_params=pltpu.CompilerParams(
            collective_id=0, has_side_effects=True, vmem_limit_bytes=56 * 1024 * 1024
        ),
        cost_estimate=pl.CostEstimate(
            flops=16 * DEGREE * rows * cols * width, bytes_accessed=8 * rows * width, transcendentals=0
        ),
    )(tile_pos[0, 0], vectors, tile_data, diag_blocks[0])


def solution(mesh):
    return jax.shard_map(
        functools.partial(body, mesh.shape["row"], mesh.shape["col"]),
        mesh=mesh,
        in_specs=(
            P("row", None),
            P("row", "col", None, None, None),
            P("row", "col", None, None),
            P(("row", "col"), None, None),
        ),
        out_specs=P("row", None),
        check_vma=False,
    )
```

```python
import functools

import jax
import jax.numpy as jnp
from jax import lax
from jax.experimental import pallas as pl
from jax.experimental.pallas import tpu as pltpu
from jax.sharding import PartitionSpec as P

DEGREE = 3
MESH = pl.DeviceIdType.MESH

filter_low = 0.0
filter_high = 8.0


def halves(value):
    high = value.astype(jnp.bfloat16)
    return high, (value - high.astype(jnp.float32)).astype(jnp.bfloat16)


def product(left_high, left_low, right):
    right_high, right_low = halves(right)
    dot = functools.partial(jnp.dot, preferred_element_type=jnp.float32)
    return dot(left_high, right_high) + (dot(left_high, right_low) + dot(left_low, right_high))


def mix(panels, field, left):
    count, width = field.shape
    depth = panels.shape[1] // 4
    turn = functools.partial(pltpu.roll, shift=width // 2, axis=1)
    high = field.astype(jnp.bfloat16).astype(jnp.float32)
    low = field - high
    pieces = [jnp.where(left, high, turn(low)), jnp.where(left, turn(high), low)]
    if depth > count:
        empty = jnp.zeros((depth - count, width), jnp.float32)
        pieces = [pieces[0], empty, pieces[1], empty]
    right = jnp.concatenate(pieces, axis=0).astype(jnp.bfloat16)
    both = jnp.dot(panels[...], jnp.concatenate([right, right], axis=0), preferred_element_type=jnp.float32)
    both = both + turn(both)
    count = both.shape[0] // 2
    return jnp.where(left, both[:count], both[count:])


def kernel(
    n_row, n_col, pos_hbm, vectors_hbm, tiles_hbm, diag_hbm, out_ref,
    pos, slots, slots_smem, vectors, tiles, diags, packed, dense,
    down, upward,
    col_field, row_field, final, direct, mirror, direct_in, mirror_in,
    load_sem, send_sem, recv_sem,
):
    orb = diag_hbm.shape[0]
    width = vectors.shape[1]
    stored = tiles.shape[1]
    half = n_col // 2
    rows, cols = half * orb, n_row * orb
    r, c = lax.axis_index("row"), lax.axis_index("col")
    h, m = c // half, c % half
    other = 1 - h
    partner = other * half + m
    row_peers = [lax.rem(r + d, n_row) for d in range(1, n_row)]
    col_slots = [lax.rem(m + d, half) for d in range(1, half)]
    left = lax.broadcasted_iota(jnp.int32, (1, width), 1) < width // 2

    def block(index):
        return pl.ds(pl.multiple_of(index * orb, 8), orb)

    loads = [
        pltpu.make_async_copy(pos_hbm, pos, load_sem.at[0]),
        pltpu.make_async_copy(vectors_hbm, vectors, load_sem.at[1]),
        pltpu.make_async_copy(tiles_hbm, tiles.at[0], load_sem.at[2]),
        pltpu.make_async_copy(diag_hbm, diags.at[0], load_sem.at[3]),
    ]
    for load in loads:
        load.start()

    barrier = pltpu.get_barrier_semaphore()
    for peer in row_peers:
        pl.semaphore_signal(barrier, inc=1, device_id=(peer, c), device_id_type=MESH)
    for slot in col_slots:
        pl.semaphore_signal(barrier, inc=1, device_id=(r, h * half + slot), device_id_type=MESH)
    pl.semaphore_signal(barrier, inc=1, device_id=(r, partner), device_id_type=MESH)

    def copy(kind, step, source, target, device):
        return pltpu.make_async_remote_copy(
            src_ref=source, dst_ref=target,
            send_sem=send_sem.at[kind, step], recv_sem=recv_sem.at[kind, step],
            device_id=device, device_id_type=MESH,
        )

    cut = orb // 16 * 8
    shares = ((0, cut), (cut, orb - cut))

    def region_of(kind, step):
        if kind == 0:
            return col_field.at[step, pl.ds(0, cols - orb)]
        if kind == 1:
            return direct_in.at[step]
        if kind == 2:
            return mirror_in.at[step]
        if kind == 3:
            return row_field.at[step, pl.ds(0, rows - orb)]
        if step == 0:
            return packed.at[1]
        if step == 1:
            return slots.at[1]
        size = shares[step // 2 - 1][1]
        return final.at[0, pl.ds(0, size * (half - 1 if step % 2 == 1 else 1))]

    def awaited(kind, step):
        region = region_of(kind, step)
        return copy(kind, step, region, region, (r, c))

    loads[2].wait()
    loads[3].wait()
    part = (width - 2 * orb) // 8 * 8
    for k in range(stored // 2):
        pieces = [tiles[0, 2 * k], tiles[0, 2 * k + 1]]
        if k * part < orb:
            share = min(part, orb - k * part)
            pieces.append(diags[0, :, pl.ds(k * part, share)])
            if share < part:
                pieces.append(jnp.zeros((orb, part - share), jnp.float32))
        else:
            pieces.append(jnp.zeros((orb, part), jnp.float32))
        packed[0, k] = jnp.concatenate(pieces, axis=1)
    loads[0].wait()
    at_row = lax.broadcasted_iota(jnp.int32, (n_col, 128), 0)
    at_col = lax.broadcasted_iota(jnp.int32, (n_col, 128), 1)
    table = jnp.zeros((n_col, 128), jnp.int32)
    for t in range(stored):
        table = jnp.where((at_row == pos[0, t]) & (at_col == pos[1, t]), t + 1, table)
    slots[0] = table
    own_slots = pltpu.make_async_copy(slots.at[0], slots_smem.at[0], load_sem.at[4])
    own_slots.start()
    loads[1].wait()
    top, bottom = vectors[pl.ds(0, rows), :], vectors[pl.ds(rows, rows), :]
    first = jnp.where(h == 0, top, pltpu.roll(top, width // 2, 1))
    second = jnp.where(h == 0, pltpu.roll(bottom, width // 2, 1), bottom)
    row_field[0] = jnp.where(left, first, second)
    own = row_field[0, block(m), :]
    col_field[0, block(r), :] = own

    pl.semaphore_wait(barrier, n_row + half - 1)

    copy(4, 1, slots.at[0], slots.at[1], (r, partner)).start()
    copy(4, 0, packed.at[0], packed.at[1], (r, partner)).start()
    for peer in row_peers:
        copy(0, 0, row_field.at[0, block(m)], col_field.at[0, block(r)], (peer, c)).start()

    dense[...] = jnp.zeros_like(dense)
    own_slots.wait()

    def fill(source, place):
        for a in range(2):
            def one(i, carry):
                parts = []
                for j in range(n_row):
                    slot = slots_smem[source, a * half + i, j]
                    tile = tiles[source, jnp.maximum(slot - 1, 0)]
                    parts.append(jnp.where(slot > 0, tile, 0.0))
                dense[a, block(i), pl.ds(0, cols)] = jnp.concatenate(parts, axis=1)
                return carry

            lax.fori_loop(0, half, one, 0)
            put(down, place, pl.ds(a * rows, rows), dense[a, pl.ds(0, rows), :])

    def put(panels, part, there, panel):
        depth = panel.shape[1]
        high, low = halves(panel)
        panels[there, pl.ds(pl.multiple_of(part * depth, 128), depth)] = high
        panels[there, pl.ds(pl.multiple_of((part + 2) * depth, 128), depth)] = low

    def turn(place):
        there = pl.ds(pl.multiple_of(place * cols, 16), cols)
        for a in range(2):
            put(upward, a, there, dense[a].T[:cols])

    fill(0, h)
    turn(h)
    awaited(4, 1).wait_recv()
    other_slots = pltpu.make_async_copy(slots.at[1], slots_smem.at[1], load_sem.at[5])
    other_slots.start()
    other_slots.wait()
    awaited(4, 0).wait_recv()
    pieces = []
    for k in range(stored // 2):
        pair = packed[1, k]
        tiles[1, 2 * k] = pair[:, :orb]
        tiles[1, 2 * k + 1] = pair[:, orb : 2 * orb]
        if k * part < orb:
            pieces.append(pair[:, 2 * orb : 2 * orb + min(part, orb - k * part)])
    diags[1] = jnp.concatenate(pieces, axis=1)
    fill(1, other)

    diag_left = halves(jnp.where(h == 0, diags[0], diags[1]))
    diag_right = halves(jnp.where(h == 0, diags[1], diags[0]))

    centre = 0.5 * (filter_high + filter_low)
    half_width = 0.5 * (filter_high - filter_low)

    def one_step(step, carry):
        previous, own = carry
        awaited(0, step).wait_recv()
        direct[step] = mix(down, col_field[step], left)
        for d, slot in enumerate(col_slots):
            copy(1, step, direct.at[step, block(slot)], direct_in.at[step, d], (r, h * half + slot)).start()

        @pl.when(step == 0)
        def _():
            turn(other)

        @pl.when(step > 0)
        def _():
            awaited(3, step).wait_recv()

        mirror[step] = mix(upward, row_field[step], left)
        for d, peer in enumerate(row_peers):
            copy(2, step, mirror.at[step, block(peer)], mirror_in.at[step, d], (peer, c)).start()
        image = jnp.where(left, product(*diag_left, own), product(*diag_right, own))
        image = image + direct[step, block(m), :] + mirror[step, block(r), :]
        awaited(1, step).wait_recv()
        for d in range(half - 1):
            image = image + direct_in[step, d]
        awaited(2, step).wait_recv()
        for d in range(n_row - 1):
            image = image + mirror_in[step, d]
        shifted = (image - centre * own) / half_width
        following = jnp.where(step == 0, shifted, 2.0 * shifted - previous)

        @pl.when(step < DEGREE - 1)
        def _():
            row_field[step + 1, block(m), :] = following
            col_field[step + 1, block(r), :] = following
            mine = row_field.at[step + 1, block(m)]
            for d in range(max(len(row_peers), len(col_slots))):
                if d < len(row_peers):
                    copy(0, step + 1, mine, col_field.at[step + 1, block(r)], (row_peers[d], c)).start()
                if d < len(col_slots):
                    copy(3, step + 1, mine, mine, (r, h * half + col_slots[d])).start()

        return own, following

    _, own = lax.fori_loop(0, DEGREE, one_step, (jnp.zeros_like(own), own))
    final[h, block(m), :] = own
    mine = final.at[h, block(m)]
    for kind, (start, size) in zip((2, 4), shares):
        piece = final.at[h, pl.ds(pl.multiple_of(m * orb + start, 8), size)]
        copy(4, kind, piece, piece, (r, partner)).start()
    for slot in col_slots:
        copy(3, 0, mine, mine, (r, h * half + slot)).start()
    for kind, (start, size) in zip((2, 4), shares):
        piece = final.at[other, pl.ds(pl.multiple_of(m * orb + start, 8), size)]
        awaited(4, kind).wait_recv()
        for slot in col_slots:
            copy(4, kind + 1, piece, piece, (r, h * half + slot)).start()
    awaited(3, 0).wait_recv()
    awaited(4, 3).wait_recv()
    awaited(4, 5).wait_recv()
    low, high = final[0], final[1]
    out_ref[pl.ds(0, rows), :] = jnp.where(left, low, pltpu.roll(high, width // 2, 1))
    out_ref[pl.ds(rows, rows), :] = jnp.where(left, pltpu.roll(low, width // 2, 1), high)
    for kind in range(5):
        for step in range(6 if kind == 4 else DEGREE):
            awaited(kind, step).wait_send()


def up(value, unit):
    return (value + unit - 1) // unit * unit


def body(n_row, n_col, vectors, tiles, tile_pos, diag_blocks):
    tile_data = tiles[0, 0]
    stored, orb, _ = tile_data.shape
    width = vectors.shape[1]
    half = n_col // 2
    rows, cols = half * orb, n_row * orb
    hbm = pl.BlockSpec(memory_space=pl.ANY)
    f32, bf16, i32 = jnp.float32, jnp.bfloat16, jnp.int32
    tall, broad = up(rows, 128), up(cols, 128)
    return pl.pallas_call(
        functools.partial(kernel, n_row, n_col),
        out_shape=jax.ShapeDtypeStruct((2 * rows, width), f32),
        in_specs=[hbm, hbm, hbm, hbm],
        out_specs=pl.BlockSpec(memory_space=pltpu.VMEM),
        scratch_shapes=[
            pltpu.SMEM(tile_pos.shape[2:], i32),
            pltpu.VMEM((2, n_col, 128), i32),
            pltpu.SMEM((2, n_col, 128), i32),
            pltpu.VMEM((2 * rows, width), f32),
            pltpu.VMEM((2, stored, orb, orb), f32),
            pltpu.VMEM((2, orb, orb), f32),
            pltpu.VMEM((2, stored // 2, orb, width), f32),
            pltpu.VMEM((2, tall, broad), f32),
            pltpu.VMEM((2 * rows, 4 * broad), bf16),
            pltpu.VMEM((2 * cols, 4 * tall), bf16),
            pltpu.VMEM((DEGREE, cols, width), f32),
            pltpu.VMEM((DEGREE, rows, width), f32),
            pltpu.VMEM((2, rows, width), f32),
            pltpu.VMEM((DEGREE, rows, width), f32),
            pltpu.VMEM((DEGREE, cols, width), f32),
            pltpu.VMEM((DEGREE, half - 1, orb, width), f32),
            pltpu.VMEM((DEGREE, n_row - 1, orb, width), f32),
            pltpu.SemaphoreType.DMA((6,)),
            pltpu.SemaphoreType.DMA((5, 6)),
            pltpu.SemaphoreType.DMA((5, 6)),
        ],
        compiler_params=pltpu.CompilerParams(
            collective_id=0, has_side_effects=True, vmem_limit_bytes=56 * 1024 * 1024
        ),
        cost_estimate=pl.CostEstimate(
            flops=16 * DEGREE * rows * cols * width, bytes_accessed=8 * rows * width, transcendentals=0
        ),
    )(tile_pos[0, 0], vectors, tile_data, diag_blocks[0])


def solution(mesh):
    return jax.shard_map(
        functools.partial(body, mesh.shape["row"], mesh.shape["col"]),
        mesh=mesh,
        in_specs=(
            P("row", None),
            P("row", "col", None, None, None),
            P("row", "col", None, None),
            P(("row", "col"), None, None),
        ),
        out_specs=P("row", None),
        check_vma=False,
    )
```
